128 devices in a mesh: ctx: 8 (over z_hi, x), exp: 16 (over y, z_lo, core).
Axes of the slice: x: 4, y: 4, z: 4 (z_hi: 2, z_lo: 2; z = z_hi * 2 + z_lo), core: 2. Of those that a mesh axis runs over, the one named last changes fastest.
Arguments:
- hidden_in: bfloat16 [16, 1024, 768], P('exp', 'ctx'), may hold values from -6 to 6
- out_grad: bfloat16 [16, 1024, 768], P('exp', 'ctx'), may hold values from -6 to 6
- attn_norm: float32 [768], replicated, may hold values from 0.1 to 1.9
- attn_weight: bfloat16 [3072, 768], P(('ctx', 'exp')), may hold values from -0.8660254 to 0.8660254
- bias_table: float32 [32, 12], replicated, may hold values from -4 to 4
- moe_norm: float32 [768], replicated, may hold values from 0.1 to 1.9
- router: float32 [768, 16], replicated, may hold values from -0.109375 to 0.109375
- expert_in: bfloat16 [16, 768, 3072], P('exp'), may hold values from -0.21875 to 0.21875
- expert_out: bfloat16 [16, 3072, 768], P('exp'), may hold values from -3.5 to 3.5
- expert_ids: int32 [16, 1024, 1], P('exp', 'ctx'), may hold values from 0 to 15; in each aligned block of 128 rows (0 to 127, 128 to 255, ..., all dimensions but the last counted through in order) at most 16 rows name the same one
- block_order: int32 [16, 16], P('exp'), may hold values from 0 to 15, each once within a row
Outputs:
- block_out: bfloat16 [16, 1024, 768], P('exp', 'ctx')
- input_grad: float32 [16, 1024, 768], P('exp', 'ctx')
- attn_norm_grad: float32 [768], replicated
- attn_weight_grad: float32 [3072, 768], P(('ctx', 'exp'))
- bias_table_grad: float32 [32, 12], replicated
- moe_norm_grad: float32 [768], replicated
- router_grad: float32 [768, 16], replicated
- expert_in_grad: float32 [16, 768, 3072], P('exp', 'ctx')
- expert_out_grad: float32 [16, 3072, 768], P('exp', 'ctx')
The draws below stay inside these ranges and needn't reach their ends.
Inputs may be any that keep to these rules, and one draw needn't show every extreme that they name: `expert_ids`: among the 128 stored rows of one sequence on one index of ctx, at most 16 name the same expert, and in every draw some expert is named by exactly 16 rows of some such block. `block_order`: each sequence's row names every stored block's place once.
All inputs are finite; a program needn't handle non-finite values.
Results may differ from the reference program's by a relative error of at most 0.02.
Values may be sent and summed in bfloat16 or wider, within the bound.
No kernel may reach another device: no remote copies, remote signals or barrier semaphores. Data moves between devices by JAX's collectives and lax.ppermute only.
A program may use at most 128 MiB of HBM per device.

```python
import math
import jax
import jax.numpy as jnp
import numpy as np
from jax import lax

D = 768
HEADS = 12
HEAD_DIM = 64
FF = 3072
BUCKETS = 32
TOK_DEV = 128
EXPERTS = 16
CAP = 16
SEQ = 1024
SEQS = 16
N_CTX = 8


def draw_attn_weight(key, part):
    key = jax.random.fold_in(key, 11)
    noise = jnp.clip(jax.random.normal(key, (4 * D, D), jnp.float32), -6.0, 6.0)
    row_ids = jnp.arange(4 * D)[:, None]
    scaling = jnp.where(row_ids < 3 * D, 1.0, 4.0) * D ** (-0.5)
    return (noise * scaling).astype(jnp.bfloat16)


def shard_levels(stream_key, extent, split, low, largest):
    level, own = 1.0, jax.random.fold_in(stream_key, 6)
    for dim, shards_of in split:
        heights = jnp.exp(jax.random.uniform(jax.random.fold_in(own, dim), (shards_of,), jnp.float32, low / len(split), largest / len(split)))
        level = level * jnp.repeat(heights, extent[dim] // shards_of).reshape([-1 if axis == dim else 1 for axis in range(len(extent))])
    return level


def assign_block(own_key, own, number, rows, number_of, top, bound, slope):
    ranking = jax.random.permutation(own_key, number_of)
    heavy_load, ordinary = portions_of(number_of, rows * top, bound, slope, True), portions_of(number_of, rows * top, bound, slope, False)
    places = jnp.arange(number_of)

    def named(sizes, offset_by):
        used = int((sizes > 0).sum())
        fixed = max(1, used // 4)
        shifted = fixed + (places - fixed + offset_by * (used - fixed)) % max(1, number_of - fixed)
        return jnp.zeros((number_of,), jnp.int32).at[ranking[jnp.where(places < fixed, places, shifted)]].set(jnp.asarray(sizes, jnp.int32))

    sizes = jnp.where(number % 4 == 0, named(heavy_load, number // 4), named(ordinary, number - number // 4 - 1))
    mixed = jax.random.permutation(jax.random.fold_in(own, 3), number_of)
    source_of, taker = mixed[0:number_of // 2 * 2:2], mixed[1:number_of // 2 * 2:2]
    slack = jnp.minimum(sizes[source_of] - 1, bound - sizes[taker]) // 2
    slack = jnp.where((source_of == ranking[0]) | (taker == ranking[0]) | (sizes[taker] == 0), 0, jnp.maximum(slack, 0))
    shifted = jax.random.randint(jax.random.fold_in(own, 4), (number_of // 2,), 0, 1 << 20) % (slack + 1)
    sizes = sizes.at[source_of].add(-shifted).at[taker].add(shifted)
    items = jnp.searchsorted(jnp.cumsum(sizes), jnp.arange(rows * top), side="right").astype(jnp.int32)
    grid = items.reshape(top, rows).T
    grid = grid[jax.random.permutation(jax.random.fold_in(own, 1), rows)]
    offset_by = jax.random.randint(jax.random.fold_in(own, 2), (rows, 1), 0, top)
    return jnp.take_along_axis(grid, (jnp.arange(top)[None, :] + offset_by) % top, axis=1)


def portions_of(number_of, total, limit, skew, full):
    portions = [(1 << 20) // math.isqrt(rank ** skew) + 1 for rank in range(1, number_of + 1)]
    largest = limit if full else min(limit, max(-(-total // number_of), total * portions[0] // sum(portions)))
    least = 1 if total - largest >= number_of - 1 else 0
    given, spare = [largest] + [least] * (number_of - 1), total - largest - least * (number_of - 1)
    while spare > 0:
        movable = [i for i in range(1, number_of) if given[i] < largest] or [i for i in range(1, number_of) if given[i] < limit]
        mass, remaining = sum([portions[i] for i in movable]), spare
        for i in movable:
            addition = min(limit - given[i], max(1, remaining * portions[i] // mass), spare)
            given[i] = given[i] + addition
            spare = spare - addition
    return np.array(given)


def centred(own_key, dims, spread, limit, split=(), kind=jnp.bfloat16):
    entries = spread * jax.random.normal(own_key, dims, jnp.float32)
    if split:
        entries = entries * shard_levels(own_key, dims, split, -0.22, 0.18)
    return jnp.clip(entries, -limit, limit).astype(kind)


def setup_inputs(seed: int = 0) -> dict:
    arg_keys = jax.random.split(jax.random.key(seed), 12)
    hidden_in = centred(arg_keys[0], (SEQS, SEQ, D), 1.0, 6.0, ((0, 16), (1, 8)))
    out_grad = centred(arg_keys[1], (SEQS, SEQ, D), 1.0, 6.0, ((0, 16), (1, 8)))
    attn_norm = jnp.clip(1.0 + 0.18 * jax.random.normal(arg_keys[2], (D,), jnp.float32), 0.1, 1.9)
    attn_weight = draw_attn_weight(jax.random.fold_in(arg_keys[11], 71), 0)
    bias_table = centred(arg_keys[4], (BUCKETS, HEADS), 1.0, 4.0, (), jnp.float32)
    moe_norm = jnp.clip(1.0 + 0.18 * jax.random.normal(arg_keys[5], (D,), jnp.float32), 0.1, 1.9)
    router = centred(arg_keys[6], (D, EXPERTS), (4 * D) ** -0.5, 0.109375, (), jnp.float32)
    expert_in = centred(arg_keys[7], (EXPERTS, D, FF), D ** -0.5, 0.21875, ((0, 16),))
    expert_out = centred(arg_keys[8], (EXPERTS, FF, D), (max(1, FF // (4 * EXPERTS * EXPERTS))) ** -0.5, 3.5, ((0, 16),))
    expert_ids_keys = jax.random.split(jax.random.fold_in(arg_keys[9], 1), SEQS * SEQ // TOK_DEV)
    expert_ids_turns = jax.random.permutation(jax.random.fold_in(arg_keys[9], 3), SEQS * SEQ // TOK_DEV)
    expert_ids = jax.vmap(lambda own, number: assign_block(jax.random.fold_in(arg_keys[9], 2), own, number, TOK_DEV, EXPERTS, 1, CAP, 1))(expert_ids_keys, expert_ids_turns).reshape((SEQS, SEQ, 1))
    block_order = jax.vmap(lambda own: jax.random.permutation(own, 2 * N_CTX))(jax.random.split(arg_keys[10], SEQS)).reshape((SEQS, 2 * N_CTX)).astype(jnp.int32)
    return dict(hidden_in=hidden_in, out_grad=out_grad, attn_norm=attn_norm, attn_weight=attn_weight, bias_table=bias_table, moe_norm=moe_norm, router=router, expert_in=expert_in, expert_out=expert_out, expert_ids=expert_ids, block_order=block_order)


@jax.custom_vjp
def low(v):
    return lax.optimization_barrier(v.astype(jnp.bfloat16)).astype(jnp.float32)

@jax.custom_vjp
def low_back(v):
    return v

def low_keep(v):
    return (low(v), None)

def low_pass(kept, grad):
    return (grad,)

def back_keep(v):
    return (v, None)

def back_low(kept, grad):
    return (low(grad),)
low.defvjp(low_keep, low_pass)
low_back.defvjp(back_keep, back_low)
eps_norm = 1e-06
highest = lax.Precision.HIGHEST
bucket_edges = np.array([edge if edge <= 16 else int(math.ceil(16.0 * 8.0 ** ((edge - 16) / 16.0))) for edge in range(1, 32)], np.int32)

def rms_scaled(values, gain):
    return values * lax.rsqrt(lax.optimization_barrier(jnp.mean(values * values, axis=-1, keepdims=True)) + eps_norm) * gain

def bucketed(distance):
    return jnp.searchsorted(jnp.asarray(bucket_edges), jnp.maximum(distance, 0), side='right').astype(jnp.int32)

def block_layer(inputs, attn_norm, attn_weight, bias_table, moe_norm, router, expert_in, expert_out, order, chosen):
    seq_rows = inputs.shape[0]
    half_block = TOK_DEV // 2
    row_ids = jnp.arange(seq_rows, dtype=jnp.int32)
    positions = (order[row_ids // half_block] * half_block + row_ids % half_block).astype(jnp.int32)
    stacked = attn_weight.reshape(4, D, D)
    normed = low(rms_scaled(inputs, attn_norm))
    projected = low_back(low(jnp.einsum('td,jdf->jtf', normed, stacked[:3], precision=highest)))
    queries = projected[0].reshape(seq_rows, HEADS, HEAD_DIM)
    all_keys = projected[1].reshape(seq_rows, HEADS, HEAD_DIM)
    all_values = projected[2].reshape(seq_rows, HEADS, HEAD_DIM)
    block_rows = min(512, seq_rows)

    def attend(pieces):
        query_block, query_pos = pieces
        distance = query_pos[:, None] - positions[None, :]
        raw_scores = jnp.einsum('qhe,khe->hqk', query_block, all_keys, precision=highest) * 0.125
        raw_scores = low_back(raw_scores + jnp.take(bias_table.T, bucketed(distance), axis=1))
        scores = jnp.where(distance[None] >= 0, raw_scores, -1e+30)
        probs = low(jax.nn.softmax(scores, axis=-1))
        return jnp.einsum('hqk,khe->qhe', probs, all_values, precision=highest)
    attended = lax.map(jax.checkpoint(attend), (queries.reshape(seq_rows // block_rows, block_rows, HEADS, HEAD_DIM), positions.reshape(seq_rows // block_rows, block_rows)))
    attended = low_back(low(attended.reshape(seq_rows, D)))
    attn_out = low_back(jnp.dot(attended, stacked[3], precision=highest))
    mid_stream = inputs + attn_out
    normed_two = rms_scaled(mid_stream, moe_norm)
    logits = jnp.dot(normed_two, router, precision=highest)
    picked = chosen[:, None] == jnp.arange(EXPERTS, dtype=jnp.int32)[None, :]
    gate_value = lax.optimization_barrier(jnp.sum(jnp.where(picked, jax.nn.softmax(logits, axis=-1), 0.0), axis=-1))
    ranks = jnp.cumsum(picked.astype(jnp.int32).reshape(N_CTX, TOK_DEV, EXPERTS), axis=1).reshape(seq_rows, EXPERTS) - 1
    slot_ids = lax.optimization_barrier(jnp.sum(jnp.where(picked, ranks, 0), axis=-1))
    targets = (chosen * (N_CTX * CAP) + row_ids // TOK_DEV * CAP + slot_ids).astype(jnp.int32)
    routed = low_back(low(normed_two))
    buffer_rows = jnp.zeros((EXPERTS * N_CTX * CAP, D), jnp.float32).at[targets].set(routed).reshape(EXPERTS, N_CTX * CAP, D)
    pre_act = low_back(jnp.einsum('erd,edf->erf', buffer_rows, expert_in, precision=highest))
    activated = low(jax.nn.gelu(pre_act, approximate=True))
    produced = low_back(low(jnp.einsum('erf,efd->erd', activated, expert_out, precision=highest)))
    expert_result = produced.reshape(EXPERTS * N_CTX * CAP, D)[targets]
    return mid_stream + gate_value[:, None] * expert_result

def reference(hidden_in, out_grad, attn_norm, attn_weight, bias_table, moe_norm, router, expert_in, expert_out, expert_ids, block_order):
    params = (attn_norm, attn_weight.astype(jnp.float32), bias_table, moe_norm, router, expert_in.astype(jnp.float32), expert_out.astype(jnp.float32))

    def per_sequence(totals, sequence_item):
        inputs, cotangent, order, chosen = sequence_item

        def forward(values, *weights):
            return block_layer(values, *weights, order, chosen[:, 0])
        result, pull = jax.vjp(forward, inputs.astype(jnp.float32), *params)
        grads = pull(cotangent.astype(jnp.float32))
        totals = tuple((total + grad for total, grad in zip(totals, grads[1:])))
        return (totals, (result.astype(jnp.bfloat16), grads[0]))
    zeros_init = tuple((jnp.zeros_like(param) for param in params))
    totals, (block_out, input_grad) = lax.scan(per_sequence, zeros_init, (hidden_in, out_grad, block_order, expert_ids))
    return (block_out, input_grad, totals[0], totals[1], totals[2], totals[3], totals[4], totals[5], totals[6])
```

```python
from functools import partial
import math

import jax
import jax.numpy as jnp
from jax import lax
from jax.experimental import pallas as pl
from jax.experimental.pallas import tpu as pltpu
from jax.sharding import PartitionSpec as P

f32 = jnp.float32
bf16 = jnp.bfloat16
eps_norm = 1e-06
highest = lax.Precision.HIGHEST
bucket_edges = [
    edge if edge <= 16 else int(math.ceil(16.0 * 8.0 ** ((edge - 16) / 16.0)))
    for edge in range(1, 32)
]
masked = -1e30
head_size = 64
own_heads = 3
width_own = own_heads * head_size
half_block = 64
block_count = 16
query_blocks = 8
lanes_step = 256
vmem_bytes = 56 * 1024 * 1024

offsets = [(dz, dx) for dz in range(2) for dx in range(4)]


def gather_perm(dz, dx):
    return [(4 * z + x, 4 * (z ^ dz) + (x + dx) % 4) for z in range(2) for x in range(4)]


def scatter_perm(dz, dx):
    return [(4 * z + x, 4 * (z ^ dz) + (x - dx) % 4) for z in range(2) for x in range(4)]


def dot_nt(left, right):
    return lax.dot_general(left, right, (((1,), (1,)), ((), ())), preferred_element_type=f32)


def dot_tn(left, right):
    return lax.dot_general(left, right, (((0,), (0,)), ((), ())), preferred_element_type=f32)


def dot_nn(left, right):
    return jnp.dot(left, right, preferred_element_type=f32)


def block_places(me_ref, order_ref):
    me = me_ref[0]
    z, x = me // 4, me % 4
    places = []
    for dz, dx in offsets:
        source = 4 * ((z + dz) % 2) + (x - dx + 4) % 4
        places += [order_ref[2 * source], order_ref[2 * source + 1]]
    return places


def tile_class(places, query_block, key_block):
    return jnp.clip(places[query_block] - places[key_block], -1, 3) + 1


def tile_distance(step):
    key_row = lax.broadcasted_iota(jnp.int32, (half_block, 128), 0)
    query_row = lax.broadcasted_iota(jnp.int32, (half_block, 128), 1) & (half_block - 1)
    return step * half_block + query_row - key_row


def attend_kernel(
    me_ref, order_ref, table_ref, normed_ref, wq_ref, wk_ref, wv_ref,
    out_ref, q_ref, k_ref, v_ref, log_ref, tiles_ref, scores_ref,
):
    places = block_places(me_ref, order_ref)
    first_head = (me_ref[0] % 4) * own_heads
    for head in range(own_heads):
        tiles_ref[head, 0] = jnp.full((half_block, 128), masked, f32)
        tiles_ref[head, 4] = jnp.full((half_block, 128), table_ref[31, first_head + head], f32)
    for step in range(3):
        distance = tile_distance(step)
        terms = [
            jnp.full((half_block, 128), table_ref[0, first_head + head], f32)
            for head in range(own_heads)
        ]
        for bucket, edge in enumerate(bucket_edges, 1):
            beyond = distance >= edge
            for head in range(own_heads):
                terms[head] = jnp.where(beyond, table_ref[bucket, first_head + head], terms[head])
        for head in range(own_heads):
            tiles_ref[head, step + 1] = (
                jnp.where(distance >= 0, terms[head], masked) if step == 0 else terms[head]
            )
    normed = normed_ref[...]
    k_ref[...] = dot_nn(normed, wk_ref[...]).astype(bf16)
    v_ref[...] = dot_nn(normed, wv_ref[...]).astype(bf16)
    q_ref[...] = dot_nn(normed[: query_blocks * half_block], wq_ref[...]).astype(bf16) * bf16(0.125)
    first_half = lax.broadcasted_iota(jnp.int32, (half_block, 128), 1) < half_block
    for head in range(own_heads):
        columns = slice(head * head_size, (head + 1) * head_size)
        keys, values = k_ref[:, columns], v_ref[:, columns]
        for part in range(query_blocks * half_block // lanes_step):
            lanes = slice(part * lanes_step, (part + 1) * lanes_step)
            add_bias(places, tiles_ref, scores_ref, first_half, head, part,
                     dot_nt(keys, q_ref[lanes, columns]))
            scores = scores_ref[...]
            peak = jnp.max(scores, axis=0, keepdims=True)
            raised = jnp.exp(scores - peak)
            total = jnp.sum(raised, axis=0, keepdims=True)
            probs = (raised * (1.0 / total)).astype(bf16)
            out_ref[columns, lanes] = dot_tn(values, probs).astype(bf16)
            log_ref[head, :, lanes] = peak + jnp.log(total)


def add_bias(places, tiles_ref, scores_ref, first_half, head, part, raw):
    for key_block in range(block_count):
        rows = slice(key_block * half_block, (key_block + 1) * half_block)
        for group in range(lanes_step // 128):
            lanes = slice(group * 128, (group + 1) * 128)
            query_block = part * (lanes_step // half_block) + 2 * group
            left = tile_class(places, query_block, key_block)
            right = tile_class(places, query_block + 1, key_block)
            scores_ref[rows, lanes] = raw[rows, lanes] + jnp.where(
                first_half, tiles_ref[head, left], tiles_ref[head, right]
            )


def attend_back_kernel(
    me_ref, order_ref, q_ref, k_ref, v_ref, grad_ref, log_ref, tiles_ref,
    dq_ref, dk_ref, dv_ref, table_ref, scores_ref, sums_ref,
):
    places = block_places(me_ref, order_ref)
    first_half = lax.broadcasted_iota(jnp.int32, (half_block, 128), 1) < half_block
    buckets = []
    for step in range(3):
        distance = tile_distance(step)
        counted = jnp.zeros((half_block, 128), jnp.int32)
        for edge in bucket_edges:
            counted = counted + (distance >= edge).astype(jnp.int32)
        buckets.append(counted)
    for head in range(own_heads):
        columns = slice(head * head_size, (head + 1) * head_size)
        keys, values = k_ref[:, columns], v_ref[:, columns]
        sums_ref[...] = jnp.zeros_like(sums_ref)
        key_sum = value_sum = None
        for part in range(query_blocks * half_block // lanes_step):
            lanes = slice(part * lanes_step, (part + 1) * lanes_step)
            queries, grads = q_ref[lanes, columns], grad_ref[lanes, columns]
            add_bias(places, tiles_ref, scores_ref, first_half, head, part, dot_nt(keys, queries))
            probs = jnp.exp(scores_ref[...] - log_ref[head, :, lanes])
            probs_grad = dot_nt(values, grads)
            row_dot = jnp.sum(probs * probs_grad, axis=0, keepdims=True)
            score_grad = probs * (probs_grad - row_dot)
            scores_ref[...] = score_grad
            low = score_grad.astype(bf16)
            value_part = dot_nn(probs.astype(bf16), grads)
            key_part = dot_nn(low, queries)
            value_sum = value_part if value_sum is None else value_sum + value_part
            key_sum = key_part if key_sum is None else key_sum + key_part
            dq_ref[columns, lanes] = (dot_tn(keys, low) * 0.125).astype(bf16)
            for key_block in range(block_count):
                rows = slice(key_block * half_block, (key_block + 1) * half_block)
                for group in range(lanes_step // 128):
                    query_block = part * (lanes_step // half_block) + 2 * group
                    left = tile_class(places, query_block, key_block)
                    right = tile_class(places, query_block + 1, key_block)
                    tile = scores_ref[rows, group * 128 : (group + 1) * 128]
                    sums_ref[left] += jnp.where(first_half, tile, 0.0)
                    sums_ref[right] += jnp.where(first_half, 0.0, tile)
        dk_ref[:, columns] = key_sum.astype(bf16)
        dv_ref[:, columns] = value_sum.astype(bf16)
        for bucket in range(32):
            found = [jnp.where(buckets[step] == bucket, sums_ref[step + 1], 0.0) for step in range(3)]
            if bucket == 31:
                found.append(sums_ref[4])
            table_ref[head, bucket : bucket + 1, :] = jnp.sum(sum(found), axis=0, keepdims=True)


def in_smem():
    return pl.BlockSpec(memory_space=pltpu.SMEM)


def in_vmem():
    return pl.BlockSpec(memory_space=pltpu.VMEM)


def attend(me, order, table, normed_all, wq, wk, wv):
    rows = normed_all.shape[0]
    shapes = [
        ((width_own, rows // 2), bf16),
        ((rows // 2, width_own), bf16),
        ((rows, width_own), bf16),
        ((rows, width_own), bf16),
        ((own_heads, 1, rows // 2), f32),
        ((own_heads, 5, half_block, 128), f32),
    ]
    return pl.pallas_call(
        attend_kernel,
        out_shape=[jax.ShapeDtypeStruct(shape, kind) for shape, kind in shapes],
        in_specs=[in_smem()] * 3 + [in_vmem()] * 4,
        out_specs=[in_vmem()] * len(shapes),
        scratch_shapes=[pltpu.VMEM((rows, lanes_step), f32)],
        compiler_params=pltpu.CompilerParams(vmem_limit_bytes=vmem_bytes),
        name="attend",
    )(me, order, table, normed_all, wq, wk, wv)


def attend_back(me, order, q, k, v, grads, logs, tiles):
    rows = k.shape[0]
    shapes = [
        ((width_own, rows // 2), bf16),
        ((rows, width_own), bf16),
        ((rows, width_own), bf16),
        ((own_heads, 32, 128), f32),
    ]
    return pl.pallas_call(
        attend_back_kernel,
        out_shape=[jax.ShapeDtypeStruct(shape, kind) for shape, kind in shapes],
        in_specs=[in_smem()] * 2 + [in_vmem()] * 6,
        out_specs=[in_vmem()] * len(shapes),
        scratch_shapes=[
            pltpu.VMEM((rows, lanes_step), f32),
            pltpu.VMEM((5, half_block, 128), f32),
        ],
        compiler_params=pltpu.CompilerParams(vmem_limit_bytes=vmem_bytes),
        name="attend_back",
    )(me, order, q, k, v, grads, logs, tiles)


def swap(chunks, axis):
    return lax.all_to_all(chunks, axis, split_axis=0, concat_axis=0, tiled=True)


def spread(part, axis, count):
    return swap(jnp.broadcast_to(part[None], (count,) + part.shape), axis)


def gelu(u):
    return jax.nn.gelu(u, approximate=True)


def body(
    hidden_in,
    out_grad,
    attn_norm,
    attn_weight,
    bias_table,
    moe_norm,
    router,
    expert_in,
    expert_out,
    expert_ids,
    block_order,
):
    width = attn_norm.shape[0]
    ctx_count, exp_count = 8, 16
    me = lax.axis_index("ctx")
    x_index = me % 4
    z_index = me // 4
    tokens = hidden_in.shape[1]
    expert_count = router.shape[1]
    capacity = 2 * tokens // expert_count
    me_array = me.astype(jnp.int32).reshape(1)
    order = block_order[0]

    inputs = hidden_in[0].astype(f32)
    scale_one = lax.rsqrt(jnp.mean(inputs * inputs, axis=-1, keepdims=True) + eps_norm)
    scaled_one = inputs * scale_one
    normed_low = (scaled_one * attn_norm).astype(bf16)
    normed_all = jnp.concatenate(
        [normed_low]
        + [lax.ppermute(normed_low, "ctx", gather_perm(dz, dx)) for dz, dx in offsets[1:]],
        axis=0,
    )
    shard_rows = attn_weight.shape[0]
    columns_ctx = spread(attn_weight, "ctx", ctx_count)
    qkv_own = lax.dynamic_slice_in_dim(columns_ctx[:6], x_index * width_own, width_own, 2)
    out_own = lax.dynamic_index_in_dim(columns_ctx, 6 + x_index // 2, 0, False)
    part_own = jnp.concatenate(
        [qkv_own.transpose(1, 0, 2).reshape(shard_rows, 6 * width_own), out_own], axis=1
    )
    parts_all = spread(part_own, "exp", exp_count)
    qkv_weights = (
        parts_all[:, :, : 6 * width_own]
        .reshape(exp_count, shard_rows, 3, 2, width_own)
        .transpose(2, 3, 0, 1, 4)
        .reshape(3, width, width_own)
    )
    out_weight = lax.dynamic_slice_in_dim(
        parts_all[:, :, 6 * width_own :], (x_index % 2) * 8, 8, 0
    ).reshape(width_own, width)

    attended, q, k, v, logs, tiles = attend(
        me_array, order, bias_table, normed_all, qkv_weights[0], qkv_weights[1], qkv_weights[2]
    )
    out_partial = dot_tn(attended, out_weight)
    out_blocks = out_partial.reshape(4, tokens, width)
    mid = inputs + out_blocks[0]
    out_low = out_blocks.astype(bf16)
    for dx in range(1, 4):
        mid = mid + lax.ppermute(out_low[dx], "ctx", scatter_perm(0, dx)).astype(f32)

    scale_two = lax.rsqrt(jnp.mean(mid * mid, axis=-1, keepdims=True) + eps_norm)
    scaled_two = mid * scale_two
    normed_two = scaled_two * moe_norm
    logits = jnp.dot(normed_two, router, precision=highest)
    router_prob = jax.nn.softmax(logits, axis=-1)
    chosen = expert_ids[0, :, 0]
    picked = chosen[:, None] == jnp.arange(expert_count, dtype=jnp.int32)[None, :]
    gate = jnp.sum(jnp.where(picked, router_prob, 0.0), axis=-1, keepdims=True)
    earlier = (
        jnp.arange(tokens, dtype=jnp.int32)[:, None] > jnp.arange(tokens, dtype=jnp.int32)[None, :]
    )
    same = chosen[:, None] == chosen[None, :]
    slot = jnp.sum((earlier & same).astype(jnp.int32), axis=1)
    targets = chosen * capacity + slot
    placing = (
        targets[:, None] == jnp.arange(expert_count * capacity, dtype=jnp.int32)[None, :]
    ).astype(bf16)
    cotangent = out_grad[0].astype(f32)
    sent = (gate * cotangent).astype(bf16)
    both = jnp.concatenate([normed_two.astype(bf16), sent], axis=1)
    outgoing = dot_tn(placing, both).astype(bf16).reshape(exp_count, capacity, 2 * width)
    arrived = swap(outgoing, "exp").reshape(exp_count * capacity, 2 * width)

    gathered = [arrived] + [
        lax.ppermute(arrived, "ctx", gather_perm(dz, dx)) for dz, dx in offsets[1:]
    ]

    w_in, w_out = expert_in[0], expert_out[0]
    rows_in, rows_grad = arrived[:, :width], arrived[:, width:]
    pre = dot_nn(rows_in, w_in)
    activated, gelu_pull = jax.vjp(gelu, pre)
    produced = dot_nn(activated.astype(bf16), w_out).astype(bf16)
    pre_grad = gelu_pull(dot_nt(rows_grad, w_out))[0].astype(bf16)
    row_grad = dot_nt(pre_grad, w_in).astype(bf16)
    returned = swap(
        jnp.concatenate([produced, row_grad], axis=1).reshape(exp_count, capacity, 2 * width), "exp"
    )
    home = dot_nn(placing, returned.reshape(exp_count * capacity, 2 * width))
    expert_result, rows_back = home[:, :width], home[:, width:]

    block_out = (mid + gate * expert_result).astype(bf16)[None]
    gate_grad = jnp.sum(cotangent * expert_result, axis=-1, keepdims=True)
    prob_grad = jnp.where(picked, gate_grad, 0.0)
    logit_grad = router_prob * (
        prob_grad - jnp.sum(router_prob * prob_grad, axis=-1, keepdims=True)
    )
    router_local = lax.dot_general(
        normed_two, logit_grad, (((0,), (0,)), ((), ())), precision=highest
    )
    normed_two_grad = rows_back + lax.dot_general(
        logit_grad, router, (((1,), (1,)), ((), ())), precision=highest
    )
    moe_norm_local = jnp.sum(normed_two_grad * scaled_two, axis=0)
    gained = normed_two_grad * moe_norm
    mid_grad = cotangent + scale_two * (
        gained - scaled_two * jnp.mean(gained * scaled_two, axis=-1, keepdims=True)
    )
    attn_grad = mid_grad.astype(bf16)
    attn_grad_half = jnp.concatenate(
        [attn_grad]
        + [lax.ppermute(attn_grad, "ctx", gather_perm(0, dx)) for dx in range(1, 4)],
        axis=0,
    )
    attended_grad = dot_nt(attn_grad_half, out_weight).astype(bf16)
    out_weight_grad = dot_nn(attended, attn_grad_half)
    dq, dk, dv, table_local = attend_back(
        me_array, order, q, k, v, attended_grad, logs, tiles
    )

    key_value_part = dot_nt(dk, qkv_weights[1]) + dot_nt(dv, qkv_weights[2])
    query_part = lax.dot_general(
        dq, qkv_weights[0], (((0,), (1,)), ((), ())), preferred_element_type=f32
    )
    half = query_part.shape[0]
    row_blocks = jnp.concatenate(
        [key_value_part[:half] + query_part, key_value_part[half:]], axis=0
    ).reshape(8, tokens, width)
    row_low = row_blocks.astype(bf16)
    normed_grad = row_blocks[0]
    for index, (dz, dx) in enumerate(offsets):
        if index:
            normed_grad = normed_grad + lax.ppermute(
                row_low[index], "ctx", scatter_perm(dz, dx)
            ).astype(f32)
    gained_one = normed_grad * attn_norm
    input_grad = (
        mid_grad
        + scale_one
        * (gained_one - scaled_one * jnp.mean(gained_one * scaled_one, axis=-1, keepdims=True))
    )[None]

    query_grad = lax.dot_general(
        normed_all[:half], dq, (((0,), (1,)), ((), ())), preferred_element_type=f32
    )
    qkv_grad = jnp.stack([query_grad, dot_tn(normed_all, dk), dot_tn(normed_all, dv)])
    attn_norm_local = jnp.sum(qkv_grad * qkv_weights.astype(f32), axis=(0, 2)) / attn_norm
    odd = x_index % 2
    out_low_grad = out_weight_grad.astype(bf16)
    half_width = width // 2
    kept = lax.dynamic_slice_in_dim(out_low_grad, odd * half_width, half_width, 1)
    given = lax.dynamic_slice_in_dim(out_low_grad, (1 - odd) * half_width, half_width, 1)
    pair = [(index, index ^ 1) for index in range(ctx_count)]
    taken = lax.ppermute(given, "ctx", pair)
    out_square = jnp.where(
        odd == 0,
        jnp.concatenate([kept, taken], axis=0),
        jnp.concatenate([taken, kept], axis=0),
    )
    weight_chunks = jnp.concatenate(
        [
            qkv_grad.astype(bf16)
            .reshape(6, exp_count, shard_rows, width_own)
            .transpose(1, 2, 0, 3)
            .reshape(exp_count, shard_rows, 6 * width_own),
            out_square.reshape(exp_count, shard_rows, half_width),
        ],
        axis=2,
    )
    table_grad = lax.dynamic_update_slice_in_dim(
        jnp.zeros(bias_table.shape, f32), jnp.sum(table_local, axis=-1).T, x_index * own_heads, 1
    )
    small = jnp.concatenate(
        [router_local.reshape(-1), table_grad.reshape(-1), attn_norm_local, moe_norm_local]
    )
    small_rows = 10
    chunk_width = 2 * width
    small = jnp.pad(small, (0, small_rows * chunk_width - small.shape[0])).reshape(
        small_rows, chunk_width
    )
    chunks = jnp.concatenate(
        [
            weight_chunks,
            jnp.broadcast_to(small.astype(bf16)[None], (exp_count, small_rows, chunk_width)),
        ],
        axis=1,
    )
    summed = jnp.sum(swap(chunks, "exp").astype(f32), axis=0)
    weight_sum, small_sum = summed[:shard_rows], summed[shard_rows:]
    qkv_sum = jnp.pad(
        weight_sum[:, : 6 * width_own].reshape(shard_rows, 6, width_own).transpose(1, 0, 2),
        ((0, 0), (0, 0), (0, half_width - width_own)),
    )
    out_sum = weight_sum[:, 6 * width_own :]
    to_out = jnp.where(
        jnp.arange(2, dtype=jnp.int32)[:, None, None] == x_index // 2, out_sum[None], 0.0
    )
    small_part = small_sum.reshape(-1, half_width)
    last = swap(
        jnp.concatenate(
            [
                jnp.concatenate([qkv_sum, to_out], axis=0),
                jnp.broadcast_to(small_part[None], (ctx_count,) + small_part.shape),
            ],
            axis=1,
        ),
        "ctx",
    )
    weight_last = last[:4, :shard_rows] + last[4:, :shard_rows]
    as_qkv = weight_last[:, :, :width_own].transpose(1, 0, 2).reshape(shard_rows, width)
    as_out = (weight_last[:2] + weight_last[2:]).transpose(1, 0, 2).reshape(shard_rows, width)
    attn_weight_grad = jnp.where(me < 6, as_qkv, as_out)
    small_last = jnp.sum(last[:, shard_rows:], axis=0).reshape(-1)
    router_size = router.size
    table_size = bias_table.size
    router_grad = small_last[:router_size].reshape(router.shape)
    small_rest = small_last[router_size:]
    bias_table_grad = small_rest[:table_size].reshape(bias_table.shape)
    attn_norm_grad = small_rest[table_size : table_size + width]
    moe_norm_grad = small_rest[table_size + width : table_size + 2 * width]

    hidden_own = w_in.shape[1] // ctx_count
    w_in_own = lax.dynamic_slice_in_dim(w_in, me * hidden_own, hidden_own, 1)
    w_out_own = lax.dynamic_slice_in_dim(w_out, me * hidden_own, hidden_own, 0)
    every = jnp.concatenate(gathered, axis=0)
    every_in, every_grad = every[:, :width], every[:, width:]
    pre_own = dot_nn(every_in, w_in_own)
    activated_own, own_pull = jax.vjp(gelu, pre_own)
    expert_out_grad = dot_tn(activated_own.astype(bf16), every_grad)[None]
    pre_grad_own = own_pull(dot_nt(every_grad, w_out_own))[0].astype(bf16)
    in_columns = dot_tn(every_in, pre_grad_own).reshape(ctx_count, width // ctx_count, hidden_own)
    in_low = in_columns.astype(bf16)
    expert_in_grad = lax.dynamic_update_slice_in_dim(
        jnp.zeros((width // ctx_count, ctx_count * hidden_own), f32),
        lax.dynamic_index_in_dim(in_columns, me, 0, False),
        me * hidden_own,
        1,
    )
    for step in range(1, ctx_count):
        given_rows = lax.dynamic_index_in_dim(in_low, (me + step) % ctx_count, 0, False)
        taken_rows = lax.ppermute(
            given_rows, "ctx", [(index, (index + step) % ctx_count) for index in range(ctx_count)]
        )
        source = (me - step + ctx_count) % ctx_count
        expert_in_grad = lax.dynamic_update_slice_in_dim(
            expert_in_grad, taken_rows.astype(f32), source * hidden_own, 1
        )
    return (
        block_out,
        input_grad,
        attn_norm_grad,
        attn_weight_grad,
        bias_table_grad,
        moe_norm_grad,
        router_grad,
        expert_in_grad[None],
        expert_out_grad,
    )


def solution(mesh):
    placed = (
        P("exp", "ctx", None),
        P("exp", "ctx", None),
        P(),
        P(("ctx", "exp"), None),
        P(),
        P(),
        P(),
        P("exp", None, None),
        P("exp", None, None),
        P("exp", "ctx", None),
        P("exp", None),
    )
    return jax.shard_map(
        body,
        mesh=mesh,
        in_specs=placed,
        out_specs=(
            P("exp", "ctx", None),
            P("exp", "ctx", None),
            P(),
            P(("ctx", "exp"), None),
            P(),
            P(),
            P(),
            P("exp", "ctx", None),
            P("exp", "ctx", None),
        ),
        check_vma=False,
    )
```

```python
from functools import partial
import math

import jax
import jax.numpy as jnp
from jax import lax
from jax.experimental import pallas as pl
from jax.experimental.pallas import tpu as pltpu
from jax.sharding import PartitionSpec as P

f32 = jnp.float32
bf16 = jnp.bfloat16
eps_norm = 1e-06
highest = lax.Precision.HIGHEST
bucket_edges = [
    edge if edge <= 16 else int(math.ceil(16.0 * 8.0 ** ((edge - 16) / 16.0)))
    for edge in range(1, 32)
]
masked = -1e30
head_size = 64
own_heads = 3
width_own = own_heads * head_size
half_block = 64
block_count = 16
query_blocks = 8
lanes_step = 256
vmem_bytes = 56 * 1024 * 1024

offsets = [(dz, dx) for dz in range(2) for dx in range(4)]


def gather_perm(dz, dx):
    return [(4 * z + x, 4 * (z ^ dz) + (x + dx) % 4) for z in range(2) for x in range(4)]


def scatter_perm(dz, dx):
    return [(4 * z + x, 4 * (z ^ dz) + (x - dx) % 4) for z in range(2) for x in range(4)]


def dot_nt(left, right):
    return lax.dot_general(left, right, (((1,), (1,)), ((), ())), preferred_element_type=f32)


def dot_tn(left, right):
    return lax.dot_general(left, right, (((0,), (0,)), ((), ())), preferred_element_type=f32)


def dot_nn(left, right):
    return jnp.dot(left, right, preferred_element_type=f32)


def block_places(me_ref, order_ref):
    me = me_ref[0]
    z, x = me // 4, me % 4
    places = []
    for dz, dx in offsets:
        source = 4 * ((z + dz) % 2) + (x - dx + 4) % 4
        places += [order_ref[2 * source], order_ref[2 * source + 1]]
    return places


def tile_class(places, query_block, key_block):
    return jnp.clip(places[query_block] - places[key_block], -1, 3) + 1


def tile_distance(step):
    key_row = lax.broadcasted_iota(jnp.int32, (half_block, 128), 0)
    query_row = lax.broadcasted_iota(jnp.int32, (half_block, 128), 1) & (half_block - 1)
    return step * half_block + query_row - key_row


def attend_kernel(me_ref, order_ref, table_ref, shards_ref, *refs):
    pieces, refs = refs[:8], refs[8:]
    out_ref, q_ref, k_ref, v_ref, log_ref, tiles_ref, weight_ref, project_ref, scores_ref = refs
    exp_count = shards_ref.shape[0]
    for which in range(3):
        weight_ref[which] = jnp.concatenate(
            [
                shards_ref[piece, which].astype(f32)[:, part * width_own : (part + 1) * width_own]
                for part in range(2)
                for piece in range(exp_count)
            ],
            axis=0,
        ).astype(bf16)
    first_piece = (me_ref[0] % 2) * (exp_count // 2)
    for part in range(2):
        project_ref[:, part * 2 * width_own : (part + 1) * 2 * width_own] = jnp.concatenate(
            [
                shards_ref[first_piece + piece, 3 + part].astype(f32)
                for piece in range(exp_count // 2)
            ],
            axis=0,
        ).astype(bf16)
    places = block_places(me_ref, order_ref)
    first_head = (me_ref[0] % 4) * own_heads
    for head in range(own_heads):
        tiles_ref[head, 0] = jnp.full((half_block, 128), masked, f32)
        tiles_ref[head, 4] = jnp.full((half_block, 128), table_ref[31, first_head + head], f32)
    for step in range(3):
        distance = tile_distance(step)
        terms = [
            jnp.full((half_block, 128), table_ref[0, first_head + head], f32)
            for head in range(own_heads)
        ]
        for bucket, edge in enumerate(bucket_edges, 1):
            beyond = distance >= edge
            for head in range(own_heads):
                terms[head] = jnp.where(beyond, table_ref[bucket, first_head + head], terms[head])
        for head in range(own_heads):
            tiles_ref[head, step + 1] = (
                jnp.where(distance >= 0, terms[head], masked) if step == 0 else terms[head]
            )
    for index, piece in enumerate(pieces):
        rows = slice(index * piece.shape[0], (index + 1) * piece.shape[0])
        normed = piece[...]
        k_ref[rows] = dot_nn(normed, weight_ref[1]).astype(bf16)
        v_ref[rows] = dot_nn(normed, weight_ref[2]).astype(bf16)
        if index < 4:
            q_ref[rows] = dot_nn(normed, weight_ref[0]).astype(bf16) * bf16(0.125)
    first_half = lax.broadcasted_iota(jnp.int32, (half_block, 128), 1) < half_block
    for head in range(own_heads):
        columns = slice(head * head_size, (head + 1) * head_size)
        keys, values = k_ref[:, columns], v_ref[:, columns]
        for part in range(query_blocks * half_block // lanes_step):
            lanes = slice(part * lanes_step, (part + 1) * lanes_step)
            add_bias(places, tiles_ref, scores_ref, first_half, head, part,
                     dot_nt(keys, q_ref[lanes, columns]))
            scores = scores_ref[...]
            peak = jnp.max(scores, axis=0, keepdims=True)
            raised = jnp.exp(scores - peak)
            total = jnp.sum(raised, axis=0, keepdims=True)
            probs = (raised * (1.0 / total)).astype(bf16)
            out_ref[columns, lanes] = dot_tn(values, probs).astype(bf16)
            log_ref[head, :, lanes] = peak + jnp.log(total)


def add_bias(places, tiles_ref, scores_ref, first_half, head, part, raw):
    for key_block in range(block_count):
        rows = slice(key_block * half_block, (key_block + 1) * half_block)
        for group in range(lanes_step // 128):
            lanes = slice(group * 128, (group + 1) * 128)
            query_block = part * (lanes_step // half_block) + 2 * group
            left = tile_class(places, query_block, key_block)
            right = tile_class(places, query_block + 1, key_block)
            scores_ref[rows, lanes] = raw[rows, lanes] + jnp.where(
                first_half, tiles_ref[head, left], tiles_ref[head, right]
            )


def attend_back_kernel(
    me_ref, order_ref, q_ref, k_ref, v_ref, log_ref, tiles_ref,
    weight_ref, project_ref, attended_ref, *refs,
):
    pieces, grad_pieces, refs = refs[:8], refs[8:12], refs[12:]
    chunk_ref, rows_ref, own_ref, table_ref = refs[:4]
    scores_ref, sums_ref, grad_ref, dq_ref, dk_ref, dv_ref, normed_ref = refs[4:]
    places = block_places(me_ref, order_ref)
    size = pieces[0].shape[0]
    for index, piece in enumerate(pieces):
        normed_ref[index * size : (index + 1) * size] = piece[...]
    project_grad = jnp.zeros(project_ref.shape, f32)
    for index, piece in enumerate(grad_pieces):
        rows = slice(index * size, (index + 1) * size)
        part_grad = piece[:size]
        grad_ref[rows] = dot_nt(part_grad, project_ref[...]).astype(bf16)
        project_grad = project_grad + dot_nn(attended_ref[:, rows], part_grad)
    first_half = lax.broadcasted_iota(jnp.int32, (half_block, 128), 1) < half_block
    buckets = []
    for step in range(3):
        distance = tile_distance(step)
        counted = jnp.zeros((half_block, 128), jnp.int32)
        for edge in bucket_edges:
            counted = counted + (distance >= edge).astype(jnp.int32)
        buckets.append(counted)
    for head in range(own_heads):
        columns = slice(head * head_size, (head + 1) * head_size)
        keys, values = k_ref[:, columns], v_ref[:, columns]
        sums_ref[...] = jnp.zeros_like(sums_ref)
        key_sum = value_sum = None
        for part in range(query_blocks * half_block // lanes_step):
            lanes = slice(part * lanes_step, (part + 1) * lanes_step)
            queries, grads = q_ref[lanes, columns], grad_ref[lanes, columns]
            add_bias(places, tiles_ref, scores_ref, first_half, head, part, dot_nt(keys, queries))
            probs = jnp.exp(scores_ref[...] - log_ref[head, :, lanes])
            probs_grad = dot_nt(values, grads)
            row_dot = jnp.sum(probs * probs_grad, axis=0, keepdims=True)
            score_grad = probs * (probs_grad - row_dot)
            scores_ref[...] = score_grad
            low = score_grad.astype(bf16)
            value_part = dot_nn(probs.astype(bf16), grads)
            key_part = dot_nn(low, queries)
            value_sum = value_part if value_sum is None else value_sum + value_part
            key_sum = key_part if key_sum is None else key_sum + key_part
            dq_ref[columns, lanes] = (dot_tn(keys, low) * 0.125).astype(bf16)
            for key_block in range(block_count):
                rows = slice(key_block * half_block, (key_block + 1) * half_block)
                for group in range(lanes_step // 128):
                    query_block = part * (lanes_step // half_block) + 2 * group
                    left = tile_class(places, query_block, key_block)
                    right = tile_class(places, query_block + 1, key_block)
                    tile = scores_ref[rows, group * 128 : (group + 1) * 128]
                    sums_ref[left] += jnp.where(first_half, tile, 0.0)
                    sums_ref[right] += jnp.where(first_half, 0.0, tile)
        dk_ref[:, columns] = key_sum.astype(bf16)
        dv_ref[:, columns] = value_sum.astype(bf16)
        for bucket in range(32):
            found = [jnp.where(buckets[step] == bucket, sums_ref[step + 1], 0.0) for step in range(3)]
            if bucket == 31:
                found.append(sums_ref[4])
            table_ref[head, bucket : bucket + 1, :] = jnp.sum(sum(found), axis=0, keepdims=True)

    dq, dk, dv = dq_ref[...], dk_ref[...], dv_ref[...]
    half = query_blocks * half_block
    rows_part = dot_nt(dk, weight_ref[1]) + dot_nt(dv, weight_ref[2])
    first_part = rows_part[:half] + dot_nt(dq.T, weight_ref[0])
    own_ref[...] = first_part[: own_ref.shape[0]]
    rows_ref[:half] = first_part.astype(bf16)
    rows_ref[half:] = rows_part[half:].astype(bf16)

    normed = normed_ref[...]
    exp_count = chunk_ref.shape[0]
    shard_rows = 24
    flipped = [dot_nn(dq, normed[:half]), dot_tn(dk, normed), dot_tn(dv, normed)]
    norm_sum = jnp.zeros((1, normed.shape[1]), f32)
    straight = []
    for which in range(3):
        weight_t = weight_ref[which].astype(f32).T
        norm_sum = norm_sum + jnp.sum(flipped[which] * weight_t, axis=0, keepdims=True)
        straight.append(flipped[which].T)
    first_head = (me_ref[0] % 4) * own_heads
    wide = 2 * width_own
    row = lax.broadcasted_iota(jnp.int32, (16, wide), 0)
    small_slab = jnp.zeros((16, wide), f32)
    for head in range(own_heads):
        sums = jnp.sum(table_ref[head].T, axis=0, keepdims=True)
        sums = jnp.concatenate([sums, jnp.zeros((1, wide - sums.shape[1]), f32)], axis=1)
        small_slab = jnp.where(row == first_head + head, sums, small_slab)
    for block in range(2):
        small_slab = jnp.where(
            row == 12 + block, norm_sum[:, block * wide : (block + 1) * wide], small_slab
        )
    early = sum(piece[size:].astype(f32) for piece in grad_pieces)
    early_slab = jnp.zeros((16, wide), f32)
    for index in range(5):
        for block in range(2):
            early_slab = jnp.where(
                row == 2 * index + block,
                early[index : index + 1, block * wide : (block + 1) * wide],
                early_slab,
            )
    odd = me_ref[0] % 2
    for piece in range(exp_count):
        slabs = []
        for which in range(3):
            starts = [(part * exp_count + piece) * shard_rows for part in range(2)]
            slabs.append(
                jnp.concatenate(
                    [straight[which][start : start + shard_rows] for start in starts], axis=1
                )
            )
        start = (piece % 8) * shard_rows
        mine = (odd == piece // 8).astype(f32)
        for block in range(2):
            slabs.append(
                project_grad[start : start + shard_rows, block * wide : (block + 1) * wide] * mine
            )
        chunk_ref[piece] = jnp.concatenate(slabs + [small_slab, early_slab], axis=0).astype(bf16)


def gelu_both(u):
    slope = math.sqrt(2.0 / math.pi)
    square = u * u
    bent = jnp.tanh(slope * u * (1.0 + 0.044715 * square))
    halved = 0.5 * (1.0 + bent)
    derivative = halved + 0.5 * u * (1.0 - bent * bent) * (slope * (1.0 + 0.134145 * square))
    return u * halved, derivative


def expert_kernel(rows_ref, in_ref, out_ref, result_ref, sum_ref):
    step = pl.program_id(0)
    width = in_ref.shape[0]
    rows_in, rows_grad = rows_ref[:, :width], rows_ref[:, width:]
    hidden, derivative = gelu_both(dot_nn(rows_in, in_ref[...]))
    produced = dot_nn(hidden.astype(bf16), out_ref[...])
    pre_grad = (dot_nt(rows_grad, out_ref[...]) * derivative).astype(bf16)
    row_grad = dot_nt(pre_grad, in_ref[...])

    @pl.when(step == 0)
    def _():
        sum_ref[:, :width] = produced
        sum_ref[:, width:] = row_grad

    @pl.when(step > 0)
    def _():
        sum_ref[:, :width] += produced
        sum_ref[:, width:] += row_grad

    @pl.when(step == pl.num_programs(0) - 1)
    def _():
        result_ref[...] = sum_ref[...].astype(bf16)


def expert(rows, w_in, w_out):
    count, double = rows.shape
    width, hidden = w_in.shape
    tile = hidden // 6
    return pl.pallas_call(
        expert_kernel,
        grid=(6,),
        out_shape=jax.ShapeDtypeStruct((count, double), bf16),
        in_specs=[
            pl.BlockSpec((count, double), lambda i: (0, 0)),
            pl.BlockSpec((width, tile), lambda i: (0, i)),
            pl.BlockSpec((tile, width), lambda i: (i, 0)),
        ],
        out_specs=pl.BlockSpec((count, double), lambda i: (0, 0)),
        scratch_shapes=[pltpu.VMEM((count, double), f32)],
        compiler_params=pltpu.CompilerParams(vmem_limit_bytes=vmem_bytes),
        name="expert",
    )(rows, w_in, w_out)


def expert_grads_kernel(
    me_ref, rows_a, rows_b, rows_c, rows_d, in_ref, out_ref,
    columns_ref, own_ref, other_ref,
):
    step = pl.program_id(0)
    width = in_ref.shape[0]
    in_sum = out_sum = None
    for piece in (rows_a, rows_b, rows_c, rows_d):
        rows_in, rows_grad = piece[:, :width], piece[:, width:]
        hidden, derivative = gelu_both(dot_nn(rows_in, in_ref[...]))
        pre_grad = (dot_nt(rows_grad, out_ref[...]) * derivative).astype(bf16)
        out_part = dot_tn(hidden.astype(bf16), rows_grad)
        in_part = dot_tn(rows_in, pre_grad)
        out_sum = out_part if out_sum is None else out_sum + out_part
        in_sum = in_part if in_sum is None else in_sum + in_part
    count = columns_ref.shape[0]
    in_rows = width // count
    columns_ref[...] = in_sum.astype(bf16).reshape(count, in_rows, in_sum.shape[1])

    @pl.when(step == me_ref[0] // 4)
    def _():
        own_ref[...] = out_sum

    @pl.when(step != me_ref[0] // 4)
    def _():
        other_ref[...] = out_sum.astype(bf16)


def expert_grads(me, pieces, w_in, w_out):
    count, double = pieces[0].shape
    width, hidden = w_in.shape
    tile = hidden // 8
    in_rows = width // 8
    return pl.pallas_call(
        expert_grads_kernel,
        grid_spec=pltpu.PrefetchScalarGridSpec(
            num_scalar_prefetch=1,
            grid=(2,),
            in_specs=[pl.BlockSpec((count, double), lambda i, me: (0, 0))] * 4
            + [
                pl.BlockSpec((width, tile), lambda i, me: (0, 4 * i + me[0] % 4)),
                pl.BlockSpec((tile, width), lambda i, me: (4 * i + me[0] % 4, 0)),
            ],
            out_specs=[
                pl.BlockSpec((8, in_rows, tile), lambda i, me: (0, 0, i)),
                pl.BlockSpec((tile, width), lambda i, me: (0, 0)),
                pl.BlockSpec((tile, width), lambda i, me: (0, 0)),
            ],
        ),
        out_shape=[
            jax.ShapeDtypeStruct((8, in_rows, 2 * tile), bf16),
            jax.ShapeDtypeStruct((tile, width), f32),
            jax.ShapeDtypeStruct((tile, width), bf16),
        ],
        compiler_params=pltpu.CompilerParams(vmem_limit_bytes=vmem_bytes),
        name="expert_grads",
    )(me, *pieces, w_in, w_out)


def in_smem():
    return pl.BlockSpec(memory_space=pltpu.SMEM)


def in_vmem():
    return pl.BlockSpec(memory_space=pltpu.VMEM)


def attend(me, order, table, shards, pieces):
    rows = 8 * pieces[0].shape[0]
    width = pieces[0].shape[1]
    shapes = [
        ((width_own, rows // 2), bf16),
        ((rows // 2, width_own), bf16),
        ((rows, width_own), bf16),
        ((rows, width_own), bf16),
        ((own_heads, 1, rows // 2), f32),
        ((own_heads, 5, half_block, 128), f32),
        ((3, width, width_own), bf16),
        ((width_own, width), bf16),
    ]
    return pl.pallas_call(
        attend_kernel,
        out_shape=[jax.ShapeDtypeStruct(shape, kind) for shape, kind in shapes],
        in_specs=[in_smem()] * 3 + [in_vmem()] * 9,
        out_specs=[in_vmem()] * len(shapes),
        scratch_shapes=[pltpu.VMEM((rows, lanes_step), f32)],
        compiler_params=pltpu.CompilerParams(vmem_limit_bytes=vmem_bytes),
        name="attend",
    )(me, order, table, shards, *pieces)


def attend_back(me, order, q, k, v, logs, tiles, weights, project, attended, pieces, grads):
    rows, width = k.shape[0], project.shape[1]
    half = rows // 2
    shapes = [
        ((16, 152, 2 * width_own), bf16),
        ((rows, width), bf16),
        ((128, width), f32),
        ((own_heads, 32, 128), f32),
    ]
    return pl.pallas_call(
        attend_back_kernel,
        out_shape=[jax.ShapeDtypeStruct(shape, kind) for shape, kind in shapes],
        in_specs=[in_smem()] * 2 + [in_vmem()] * 20,
        out_specs=[in_vmem()] * len(shapes),
        scratch_shapes=[
            pltpu.VMEM((rows, lanes_step), f32),
            pltpu.VMEM((5, half_block, 128), f32),
            pltpu.VMEM((half, width_own), bf16),
            pltpu.VMEM((width_own, half), bf16),
            pltpu.VMEM((rows, width_own), bf16),
            pltpu.VMEM((rows, width_own), bf16),
            pltpu.VMEM((rows, width), bf16),
        ],
        compiler_params=pltpu.CompilerParams(vmem_limit_bytes=vmem_bytes),
        name="attend_back",
    )(me, order, q, k, v, logs, tiles, weights, project, attended, *pieces, *grads)


def swap(chunks, axis):
    return lax.all_to_all(chunks, axis, split_axis=0, concat_axis=0, tiled=True)


def spread(part, axis, count):
    return swap(jnp.broadcast_to(part[None], (count,) + part.shape), axis)


def gelu(u):
    return jax.nn.gelu(u, approximate=True)


def body(
    hidden_in,
    out_grad,
    attn_norm,
    attn_weight,
    bias_table,
    moe_norm,
    router,
    expert_in,
    expert_out,
    expert_ids,
    block_order,
):
    width = attn_norm.shape[0]
    ctx_count, exp_count = 8, 16
    me = lax.axis_index("ctx")
    x_index = me % 4
    z_index = me // 4
    tokens = hidden_in.shape[1]
    expert_count = router.shape[1]
    capacity = 2 * tokens // expert_count
    me_array = me.astype(jnp.int32).reshape(1)
    order = block_order[0]

    inputs = hidden_in[0].astype(f32)
    scale_one = lax.rsqrt(jnp.mean(inputs * inputs, axis=-1, keepdims=True) + eps_norm)
    scaled_one = inputs * scale_one
    normed_low = (scaled_one * attn_norm).astype(bf16)
    pieces = [normed_low] + [
        lax.ppermute(normed_low, "ctx", gather_perm(dz, dx)) for dz, dx in offsets[1:]
    ]
    shard_rows = attn_weight.shape[0]
    by_ctx = spread(attn_weight, "ctx", ctx_count)
    qkv_own = lax.dynamic_slice_in_dim(by_ctx[:6], x_index * width_own, width_own, 2)
    out_own = lax.dynamic_index_in_dim(by_ctx, 6 + x_index // 2, 0, False)
    wide = 2 * width_own
    part_own = jnp.stack(
        [jnp.concatenate([qkv_own[2 * which], qkv_own[2 * which + 1]], axis=1) for which in range(3)]
        + [out_own[:, :wide], out_own[:, wide:]]
    )
    part_own, *pieces[1:5] = lax.optimization_barrier((part_own, *pieces[1:5]))
    by_exp = spread(part_own, "exp", exp_count)
    attended, q, k, v, logs, tiles, qkv_weights, out_weight = attend(
        me_array, order, bias_table, by_exp, pieces
    )
    out_partial = dot_tn(attended, out_weight)
    out_blocks = out_partial.reshape(4, tokens, width)
    mid = inputs + out_blocks[0]
    out_low = out_blocks.astype(bf16)
    for dx in range(1, 4):
        mid = mid + lax.ppermute(out_low[dx], "ctx", scatter_perm(0, dx)).astype(f32)

    scale_two = lax.rsqrt(jnp.mean(mid * mid, axis=-1, keepdims=True) + eps_norm)
    scaled_two = mid * scale_two
    normed_two = scaled_two * moe_norm
    logits = jnp.dot(normed_two, router, precision=highest)
    router_prob = jax.nn.softmax(logits, axis=-1)
    chosen = expert_ids[0, :, 0]
    picked = chosen[:, None] == jnp.arange(expert_count, dtype=jnp.int32)[None, :]
    gate = jnp.sum(jnp.where(picked, router_prob, 0.0), axis=-1, keepdims=True)
    earlier = (
        jnp.arange(tokens, dtype=jnp.int32)[:, None] > jnp.arange(tokens, dtype=jnp.int32)[None, :]
    )
    same = chosen[:, None] == chosen[None, :]
    slot = jnp.sum((earlier & same).astype(jnp.int32), axis=1)
    targets = chosen * capacity + slot
    placing = (
        targets[:, None] == jnp.arange(expert_count * capacity, dtype=jnp.int32)[None, :]
    ).astype(bf16)
    cotangent = out_grad[0].astype(f32)
    sent = (gate * cotangent).astype(bf16)
    both = jnp.concatenate([normed_two.astype(bf16), sent], axis=1)
    outgoing = dot_tn(placing, both).astype(bf16).reshape(exp_count, capacity, 2 * width)
    arrived = swap(outgoing, "exp").reshape(exp_count * capacity, 2 * width)

    gathered = [arrived] + [
        lax.ppermute(arrived, "ctx", gather_perm(0, dx)) for dx in range(1, 4)
    ]

    w_in, w_out = expert_in[0], expert_out[0]
    returned = swap(expert(arrived, w_in, w_out).reshape(exp_count, capacity, 2 * width), "exp")
    returned, *gathered[1:] = lax.optimization_barrier((returned, *gathered[1:]))
    home = dot_nn(placing, returned.reshape(exp_count * capacity, 2 * width))
    expert_result, rows_back = home[:, :width], home[:, width:]

    block_out = (mid + gate * expert_result).astype(bf16)[None]
    gate_grad = jnp.sum(cotangent * expert_result, axis=-1, keepdims=True)
    prob_grad = jnp.where(picked, gate_grad, 0.0)
    logit_grad = router_prob * (
        prob_grad - jnp.sum(router_prob * prob_grad, axis=-1, keepdims=True)
    )
    router_local = lax.dot_general(
        logit_grad, normed_two, (((0,), (0,)), ((), ())), precision=highest
    )
    normed_two_grad = rows_back + lax.dot_general(
        logit_grad, router, (((1,), (1,)), ((), ())), precision=highest
    )
    moe_norm_local = jnp.sum(normed_two_grad * scaled_two, axis=0)
    gained = normed_two_grad * moe_norm
    mid_grad = cotangent + scale_two * (
        gained - scaled_two * jnp.mean(gained * scaled_two, axis=-1, keepdims=True)
    )
    attn_grad = mid_grad.astype(bf16)
    quarter = jnp.arange(width, dtype=jnp.int32)[None] // width_own
    attn_grads = []
    for dx in range(4):
        target = (x_index + dx) % 4
        small = jnp.concatenate(
            [
                lax.dynamic_slice_in_dim(router_local, target * 4, 4, 0),
                jnp.where(quarter == target, moe_norm_local[None], 0.0),
                jnp.zeros((11, width), f32),
            ],
            axis=0,
        )
        part = jnp.concatenate([attn_grad, small.astype(bf16)], axis=0)
        attn_grads.append(lax.ppermute(part, "ctx", gather_perm(0, dx)) if dx else part)

    in_columns, out_own_grad, out_other_grad = expert_grads(
        me_array, gathered, w_in, w_out
    )
    in_columns, out_other_grad, *attn_grads = lax.optimization_barrier(
        (in_columns, out_other_grad, *attn_grads)
    )
    columns_last = swap(in_columns, "ctx")
    out_taken = lax.ppermute(out_other_grad, "ctx", gather_perm(1, 0))
    in_rows = width // ctx_count
    hidden_own = w_in.shape[1] // ctx_count
    chunks, row_low, row_own, _ = attend_back(
        me_array, order, q, k, v, logs, tiles, qkv_weights, out_weight, attended, pieces, attn_grads
    )
    chunks, columns_last, out_taken = lax.optimization_barrier((chunks, columns_last, out_taken))
    summed = jnp.sum(swap(chunks, "exp").astype(f32), axis=0)
    expert_in_grad = (
        columns_last
        .astype(f32)
        .reshape(2, 4, in_rows, 2, hidden_own)
        .sum(0)
        .transpose(1, 2, 0, 3)
        .reshape(in_rows, ctx_count * hidden_own)
    )
    expert_out_grad = (out_own_grad + out_taken.astype(f32))[None]

    row_low = row_low.reshape(8, tokens, width)
    row_parts = [
        lax.ppermute(row_low[index], "ctx", scatter_perm(dz, dx))
        for index, (dz, dx) in enumerate(offsets)
        if index
    ]
    *row_parts, _ = lax.optimization_barrier((*row_parts, summed[:1, :1]))
    normed_grad = row_own
    for part in row_parts:
        normed_grad = normed_grad + part.astype(f32)
    gained_one = normed_grad * attn_norm
    input_grad = (
        mid_grad
        + scale_one
        * (gained_one - scaled_one * jnp.mean(gained_one * scaled_one, axis=-1, keepdims=True))
    )[None]

    weight_rows = 5 * shard_rows
    low = summed.astype(bf16)
    qkv_sum = jnp.stack(
        [
            low[which * shard_rows : (which + 1) * shard_rows, part * width_own : (part + 1) * width_own]
            for which in range(3)
            for part in range(2)
        ]
    )
    to_qkv = jnp.pad(qkv_sum, ((0, 0), (0, shard_rows), (0, width_own)))
    to_out = jnp.where(
        jnp.arange(2, dtype=jnp.int32)[:, None, None] == x_index // 2,
        low[3 * shard_rows : weight_rows][None],
        bf16(0),
    )
    weight_part = jnp.concatenate([to_qkv, to_out], axis=0)
    small_part = low[weight_rows:]
    last = swap(
        jnp.concatenate(
            [weight_part, jnp.broadcast_to(small_part[None], (ctx_count,) + small_part.shape)],
            axis=1,
        ),
        "ctx",
    )
    weight_last = last[:, : 2 * shard_rows].astype(f32)
    as_qkv = (
        (weight_last[:4, :shard_rows, :width_own] + weight_last[4:, :shard_rows, :width_own])
        .transpose(1, 0, 2)
        .reshape(shard_rows, width)
    )
    as_out = jnp.sum(weight_last, axis=0)
    as_out = jnp.concatenate([as_out[:shard_rows], as_out[shard_rows:]], axis=1)
    attn_weight_grad = jnp.where(me < 6, as_qkv, as_out)
    small_last = last[:, 2 * shard_rows :].astype(f32)
    table_last = jnp.sum(small_last[:, :16], axis=0)
    bias_table_grad = table_last[: bias_table.shape[1], : bias_table.shape[0]].T
    attn_norm_grad = table_last[12:14].reshape(-1) / attn_norm
    early_last = small_last[:4, 16:26] + small_last[4:, 16:26]
    early_last = early_last.reshape(4, 5, width)
    router_grad = early_last[:, :4].reshape(expert_count, width).T
    moe_norm_grad = jnp.sum(early_last[:, 4], axis=0)
    return (
        block_out,
        input_grad,
        attn_norm_grad,
        attn_weight_grad,
        bias_table_grad,
        moe_norm_grad,
        router_grad,
        expert_in_grad[None],
        expert_out_grad,
    )


def solution(mesh):
    placed = (
        P("exp", "ctx", None),
        P("exp", "ctx", None),
        P(),
        P(("ctx", "exp"), None),
        P(),
        P(),
        P(),
        P("exp", None, None),
        P("exp", None, None),
        P("exp", "ctx", None),
        P("exp", None),
    )
    return jax.shard_map(
        body,
        mesh=mesh,
        in_specs=placed,
        out_specs=(
            P("exp", "ctx", None),
            P("exp", "ctx", None),
            P(),
            P(("ctx", "exp"), None),
            P(),
            P(),
            P(),
            P("exp", "ctx", None),
            P("exp", "ctx", None),
        ),
        check_vma=False,
    )
```

```python
from functools import partial
import math

import jax
import jax.numpy as jnp
from jax import lax
from jax.experimental import pallas as pl
from jax.experimental.pallas import tpu as pltpu
from jax.sharding import PartitionSpec as P

f32 = jnp.float32
bf16 = jnp.bfloat16
eps_norm = 1e-06
highest = lax.Precision.HIGHEST
bucket_edges = [
    edge if edge <= 16 else int(math.ceil(16.0 * 8.0 ** ((edge - 16) / 16.0)))
    for edge in range(1, 32)
]
masked = -1e30
head_size = 64
own_heads = 3
width_own = own_heads * head_size
half_block = 64
block_count = 16
query_blocks = 8
lanes_step = 256
vmem_bytes = 56 * 1024 * 1024

offsets = [(dz, dx) for dz in range(2) for dx in range(4)]


def gather_perm(dz, dx):
    return [(4 * z + x, 4 * (z ^ dz) + (x + dx) % 4) for z in range(2) for x in range(4)]


def scatter_perm(dz, dx):
    return [(4 * z + x, 4 * (z ^ dz) + (x - dx) % 4) for z in range(2) for x in range(4)]


def dot_nt(left, right):
    return lax.dot_general(left, right, (((1,), (1,)), ((), ())), preferred_element_type=f32)


def dot_tn(left, right):
    return lax.dot_general(left, right, (((0,), (0,)), ((), ())), preferred_element_type=f32)


def dot_nn(left, right):
    return jnp.dot(left, right, preferred_element_type=f32)


def block_places(me_ref, order_ref):
    me = me_ref[0]
    z, x = me // 4, me % 4
    places = []
    for dz, dx in offsets:
        source = 4 * ((z + dz) % 2) + (x - dx + 4) % 4
        places += [order_ref[2 * source], order_ref[2 * source + 1]]
    return places


def tile_class(places, query_block, key_block):
    return jnp.clip(places[query_block] - places[key_block], -1, 3) + 1


def tile_distance(step):
    key_row = lax.broadcasted_iota(jnp.int32, (half_block, 128), 0)
    query_row = lax.broadcasted_iota(jnp.int32, (half_block, 128), 1) & (half_block - 1)
    return step * half_block + query_row - key_row


def attend_kernel(me_ref, order_ref, table_ref, shards_ref, *refs):
    pieces, refs = refs[:8], refs[8:]
    out_ref, q_ref, k_ref, v_ref, log_ref, tiles_ref, weight_ref, project_ref, scores_ref = refs
    exp_count = shards_ref.shape[0]
    for which in range(3):
        weight_ref[which] = jnp.concatenate(
            [
                shards_ref[piece, which].astype(f32)[:, part * width_own : (part + 1) * width_own]
                for part in range(2)
                for piece in range(exp_count)
            ],
            axis=0,
        ).astype(bf16)
    first_piece = (me_ref[0] % 2) * (exp_count // 2)
    for part in range(2):
        project_ref[:, part * 2 * width_own : (part + 1) * 2 * width_own] = jnp.concatenate(
            [
                shards_ref[first_piece + piece, 3 + part].astype(f32)
                for piece in range(exp_count // 2)
            ],
            axis=0,
        ).astype(bf16)
    places = block_places(me_ref, order_ref)
    first_head = (me_ref[0] % 4) * own_heads
    for head in range(own_heads):
        tiles_ref[head, 0] = jnp.full((half_block, 128), masked, f32)
        tiles_ref[head, 4] = jnp.full((half_block, 128), table_ref[31, first_head + head], f32)
    for step in range(3):
        distance = tile_distance(step)
        terms = [
            jnp.full((half_block, 128), table_ref[0, first_head + head], f32)
            for head in range(own_heads)
        ]
        for bucket, edge in enumerate(bucket_edges, 1):
            beyond = distance >= edge
            for head in range(own_heads):
                terms[head] = jnp.where(beyond, table_ref[bucket, first_head + head], terms[head])
        for head in range(own_heads):
            tiles_ref[head, step + 1] = (
                jnp.where(distance >= 0, terms[head], masked) if step == 0 else terms[head]
            )
    for index, piece in enumerate(pieces):
        rows = slice(index * piece.shape[0], (index + 1) * piece.shape[0])
        normed = piece[...]
        k_ref[rows] = dot_nn(normed, weight_ref[1]).astype(bf16)
        v_ref[rows] = dot_nn(normed, weight_ref[2]).astype(bf16)
        if index < 4:
            q_ref[rows] = dot_nn(normed, weight_ref[0]).astype(bf16) * bf16(0.125)
    first_half = lax.broadcasted_iota(jnp.int32, (half_block, 128), 1) < half_block
    for head in range(own_heads):
        columns = slice(head * head_size, (head + 1) * head_size)
        keys, values = k_ref[:, columns], v_ref[:, columns]
        for part in range(query_blocks * half_block // lanes_step):
            lanes = slice(part * lanes_step, (part + 1) * lanes_step)
            add_bias(places, tiles_ref, scores_ref, first_half, head, part,
                     dot_nt(keys, q_ref[lanes, columns]))
            scores = scores_ref[...]
            peak = jnp.max(scores, axis=0, keepdims=True)
            raised = jnp.exp(scores - peak)
            total = jnp.sum(raised, axis=0, keepdims=True)
            probs = (raised * (1.0 / total)).astype(bf16)
            out_ref[columns, lanes] = dot_tn(values, probs).astype(bf16)
            log_ref[head, :, lanes] = peak + jnp.log(total)


def add_bias(places, tiles_ref, scores_ref, first_half, head, part, raw):
    for key_block in range(block_count):
        rows = slice(key_block * half_block, (key_block + 1) * half_block)
        for group in range(lanes_step // 128):
            lanes = slice(group * 128, (group + 1) * 128)
            query_block = part * (lanes_step // half_block) + 2 * group
            left = tile_class(places, query_block, key_block)
            right = tile_class(places, query_block + 1, key_block)
            scores_ref[rows, lanes] = raw[rows, lanes] + jnp.where(
                first_half, tiles_ref[head, left], tiles_ref[head, right]
            )


def attend_back_kernel(
    me_ref, order_ref, q_ref, k_ref, v_ref, log_ref, tiles_ref, project_ref, *refs,
):
    grad_pieces, refs = refs[:4], refs[4:]
    dq_ref, dk_ref, dv_ref, query_ref, keep_ref, give_ref, table_ref = refs[:7]
    scores_ref, sums_ref, grad_ref = refs[7:]
    places = block_places(me_ref, order_ref)
    size = query_blocks * half_block // 4
    for index, piece in enumerate(grad_pieces):
        rows = slice(index * size, (index + 1) * size)
        grad_ref[rows] = dot_nt(piece[:size], project_ref[...]).astype(bf16)
    first_half = lax.broadcasted_iota(jnp.int32, (half_block, 128), 1) < half_block
    buckets = []
    for step in range(3):
        distance = tile_distance(step)
        counted = jnp.zeros((half_block, 128), jnp.int32)
        for edge in bucket_edges:
            counted = counted + (distance >= edge).astype(jnp.int32)
        buckets.append(counted)
    for head in range(own_heads):
        columns = slice(head * head_size, (head + 1) * head_size)
        keys, values = k_ref[:, columns], v_ref[:, columns]
        sums_ref[...] = jnp.zeros_like(sums_ref)
        key_sum = value_sum = None
        for part in range(query_blocks * half_block // lanes_step):
            lanes = slice(part * lanes_step, (part + 1) * lanes_step)
            queries, grads = q_ref[lanes, columns], grad_ref[lanes, columns]
            add_bias(places, tiles_ref, scores_ref, first_half, head, part, dot_nt(keys, queries))
            probs = jnp.exp(scores_ref[...] - log_ref[head, :, lanes])
            probs_grad = dot_nt(values, grads)
            row_dot = jnp.sum(probs * probs_grad, axis=0, keepdims=True)
            score_grad = probs * (probs_grad - row_dot)
            scores_ref[...] = score_grad
            low = score_grad.astype(bf16)
            value_part = dot_nn(probs.astype(bf16), grads)
            key_part = dot_nn(low, queries)
            value_sum = value_part if value_sum is None else value_sum + value_part
            key_sum = key_part if key_sum is None else key_sum + key_part
            dq_ref[columns, lanes] = (dot_tn(keys, low) * 0.125).astype(bf16)
            for key_block in range(block_count):
                rows = slice(key_block * half_block, (key_block + 1) * half_block)
                for group in range(lanes_step // 128):
                    query_block = part * (lanes_step // half_block) + 2 * group
                    left = tile_class(places, query_block, key_block)
                    right = tile_class(places, query_block + 1, key_block)
                    tile = scores_ref[rows, group * 128 : (group + 1) * 128]
                    sums_ref[left] += jnp.where(first_half, tile, 0.0)
                    sums_ref[right] += jnp.where(first_half, 0.0, tile)
        dk_ref[:, columns] = key_sum.astype(bf16)
        dv_ref[:, columns] = value_sum.astype(bf16)
        for bucket in range(32):
            found = [jnp.where(buckets[step] == bucket, sums_ref[step + 1], 0.0) for step in range(3)]
            if bucket == 31:
                found.append(sums_ref[4])
            table_ref[head, bucket : bucket + 1, :] = jnp.sum(sum(found), axis=0, keepdims=True)

    dq, dk, dv = dq_ref[...], dk_ref[...], dv_ref[...]
    half = query_blocks * half_block
    query_ref[...] = dq.T
    keys_values = jnp.concatenate([dk.astype(f32), dv.astype(f32)], axis=1).astype(bf16)
    keep_ref[...] = keys_values[:half]
    give_ref[...] = keys_values[half:]


def pieces_kernel(
    me_ref, dq_ref, dk_ref, dv_ref, table_ref, weight_ref, attended_ref, *refs,
):
    pieces, grad_pieces, chunk_ref, normed_ref = refs[:8], refs[8:12], refs[12], refs[13]
    size = pieces[0].shape[0]
    for index, piece in enumerate(pieces):
        normed_ref[index * size : (index + 1) * size] = piece[...]
    project_grad = jnp.zeros((width_own, normed_ref.shape[1]), f32)
    for index, piece in enumerate(grad_pieces):
        rows = slice(index * size, (index + 1) * size)
        project_grad = project_grad + dot_nn(attended_ref[:, rows], piece[:size])
    normed = normed_ref[...]
    half = normed.shape[0] // 2
    exp_count = chunk_ref.shape[0]
    shard_rows = 24
    flipped = [
        dot_nn(dq_ref[...], normed[:half]),
        dot_tn(dk_ref[...], normed),
        dot_tn(dv_ref[...], normed),
    ]
    norm_sum = jnp.zeros((1, normed.shape[1]), f32)
    straight = []
    for which in range(3):
        weight_t = weight_ref[which].astype(f32).T
        norm_sum = norm_sum + jnp.sum(flipped[which] * weight_t, axis=0, keepdims=True)
        straight.append(flipped[which].T)
    wide = 2 * width_own
    row = lax.broadcasted_iota(jnp.int32, (16, wide), 0)
    heads = [jnp.sum(table_ref[head].T, axis=0, keepdims=True) for head in range(own_heads)]
    table_row = jnp.concatenate(
        [
            heads[head] * (me_ref[0] % 4 == group).astype(f32)
            for group in range(4)
            for head in range(own_heads)
        ],
        axis=1,
    )
    small_rows = [table_row, norm_sum[:, :wide], norm_sum[:, wide:]]
    early = sum(piece[size:].astype(f32) for piece in grad_pieces)
    for index in range(5):
        for block in range(2):
            small_rows.append(early[index : index + 1, block * wide : (block + 1) * wide])
    small_slab = jnp.zeros((16, wide), f32)
    for index, small_row in enumerate(small_rows):
        small_slab = jnp.where(row == index, small_row, small_slab)
    odd = me_ref[0] % 2
    for piece in range(exp_count):
        slabs = []
        for which in range(3):
            starts = [(part * exp_count + piece) * shard_rows for part in range(2)]
            slabs.append(
                jnp.concatenate(
                    [straight[which][start : start + shard_rows] for start in starts], axis=1
                )
            )
        start = (piece % 8) * shard_rows
        mine = (odd == piece // 8).astype(f32)
        for block in range(2):
            slabs.append(
                project_grad[start : start + shard_rows, block * wide : (block + 1) * wide] * mine
            )
        chunk_ref[piece] = jnp.concatenate(slabs + [small_slab], axis=0).astype(bf16)


def rows_kernel(query_ref, keep_ref, taken_ref, weight_ref, own_ref, *low_refs):
    size = own_ref.shape[0]
    for index in range(4):
        rows = slice(index * size, (index + 1) * size)
        both = keep_ref[rows].astype(f32) + taken_ref[rows].astype(f32)
        part = dot_nt(query_ref[rows], weight_ref[0])
        part = part + dot_nt(both[:, :width_own].astype(bf16), weight_ref[1])
        part = part + dot_nt(both[:, width_own:].astype(bf16), weight_ref[2])
        if index:
            low_refs[index - 1][...] = part.astype(bf16)
        else:
            own_ref[...] = part


def rows_grad(query, keep, taken, weights):
    size, width = query.shape[0] // 4, weights.shape[1]
    return pl.pallas_call(
        rows_kernel,
        out_shape=[jax.ShapeDtypeStruct((size, width), kind) for kind in (f32, bf16, bf16, bf16)],
        in_specs=[in_vmem()] * 4,
        out_specs=[in_vmem()] * 4,
        compiler_params=pltpu.CompilerParams(vmem_limit_bytes=vmem_bytes),
        name="rows_grad",
    )(query, keep, taken, weights)


def place_kernel(columns_ref, placed_ref):
    tile = columns_ref.shape[2] // 2
    for source in range(4):
        both = columns_ref[source].astype(f32) + columns_ref[4 + source].astype(f32)
        for part in range(2):
            start = (4 * part + source) * tile
            placed_ref[:, start : start + tile] = both[:, part * tile : (part + 1) * tile]


def place(columns):
    count, rows, double = columns.shape
    return pl.pallas_call(
        place_kernel,
        out_shape=jax.ShapeDtypeStruct((rows, count * double // 2), f32),
        in_specs=[in_vmem()],
        out_specs=in_vmem(),
        compiler_params=pltpu.CompilerParams(vmem_limit_bytes=vmem_bytes),
        name="place",
    )(columns)


def gelu_both(u):
    slope = math.sqrt(2.0 / math.pi)
    square = u * u
    bent = jnp.tanh(slope * u * (1.0 + 0.044715 * square))
    halved = 0.5 * (1.0 + bent)
    derivative = halved + 0.5 * u * (1.0 - bent * bent) * (slope * (1.0 + 0.134145 * square))
    return u * halved, derivative


def expert_kernel(rows_ref, in_ref, out_ref, result_ref, sum_ref):
    step = pl.program_id(0)
    width = in_ref.shape[0]
    rows_in, rows_grad = rows_ref[:, :width], rows_ref[:, width:]
    hidden, derivative = gelu_both(dot_nn(rows_in, in_ref[...]))
    produced = dot_nn(hidden.astype(bf16), out_ref[...])
    pre_grad = (dot_nt(rows_grad, out_ref[...]) * derivative).astype(bf16)
    row_grad = dot_nt(pre_grad, in_ref[...])

    @pl.when(step == 0)
    def _():
        sum_ref[:, :width] = produced
        sum_ref[:, width:] = row_grad

    @pl.when(step > 0)
    def _():
        sum_ref[:, :width] += produced
        sum_ref[:, width:] += row_grad

    @pl.when(step == pl.num_programs(0) - 1)
    def _():
        result_ref[...] = sum_ref[...].astype(bf16)


def expert(rows, w_in, w_out):
    count, double = rows.shape
    width, hidden = w_in.shape
    tile = hidden // 3
    return pl.pallas_call(
        expert_kernel,
        grid=(3,),
        out_shape=jax.ShapeDtypeStruct((count, double), bf16),
        in_specs=[
            pl.BlockSpec((count, double), lambda i: (0, 0)),
            pl.BlockSpec((width, tile), lambda i: (0, i)),
            pl.BlockSpec((tile, width), lambda i: (i, 0)),
        ],
        out_specs=pl.BlockSpec((count, double), lambda i: (0, 0)),
        scratch_shapes=[pltpu.VMEM((count, double), f32)],
        compiler_params=pltpu.CompilerParams(vmem_limit_bytes=vmem_bytes),
        name="expert",
    )(rows, w_in, w_out)


def expert_grads_kernel(
    me_ref, rows_a, rows_b, rows_c, rows_d, in_ref, out_ref,
    columns_ref, own_ref, other_ref,
):
    step = pl.program_id(0)
    width = in_ref.shape[0]
    in_sum = out_sum = None
    for piece in (rows_a, rows_b, rows_c, rows_d):
        rows_in, rows_grad = piece[:, :width], piece[:, width:]
        hidden, derivative = gelu_both(dot_nn(rows_in, in_ref[...]))
        pre_grad = (dot_nt(rows_grad, out_ref[...]) * derivative).astype(bf16)
        out_part = dot_tn(hidden.astype(bf16), rows_grad)
        in_part = dot_tn(rows_in, pre_grad)
        out_sum = out_part if out_sum is None else out_sum + out_part
        in_sum = in_part if in_sum is None else in_sum + in_part
    count = columns_ref.shape[0]
    in_rows = width // count
    columns_ref[...] = in_sum.astype(bf16).reshape(count, in_rows, in_sum.shape[1])

    @pl.when(step == me_ref[0] // 4)
    def _():
        own_ref[...] = out_sum

    @pl.when(step != me_ref[0] // 4)
    def _():
        other_ref[...] = out_sum.astype(bf16)


def expert_grads(me, pieces, w_in, w_out):
    count, double = pieces[0].shape
    width, hidden = w_in.shape
    tile = hidden // 8
    in_rows = width // 8
    return pl.pallas_call(
        expert_grads_kernel,
        grid_spec=pltpu.PrefetchScalarGridSpec(
            num_scalar_prefetch=1,
            grid=(2,),
            in_specs=[pl.BlockSpec((count, double), lambda i, me: (0, 0))] * 4
            + [
                pl.BlockSpec((width, tile), lambda i, me: (0, 4 * i + me[0] % 4)),
                pl.BlockSpec((tile, width), lambda i, me: (4 * i + me[0] % 4, 0)),
            ],
            out_specs=[
                pl.BlockSpec((8, in_rows, tile), lambda i, me: (0, 0, i)),
                pl.BlockSpec((tile, width), lambda i, me: (0, 0)),
                pl.BlockSpec((tile, width), lambda i, me: (0, 0)),
            ],
        ),
        out_shape=[
            jax.ShapeDtypeStruct((8, in_rows, 2 * tile), bf16),
            jax.ShapeDtypeStruct((tile, width), f32),
            jax.ShapeDtypeStruct((tile, width), bf16),
        ],
        compiler_params=pltpu.CompilerParams(vmem_limit_bytes=vmem_bytes),
        name="expert_grads",
    )(me, *pieces, w_in, w_out)


def in_smem():
    return pl.BlockSpec(memory_space=pltpu.SMEM)


def in_vmem():
    return pl.BlockSpec(memory_space=pltpu.VMEM)


def attend(me, order, table, shards, pieces):
    rows = 8 * pieces[0].shape[0]
    width = pieces[0].shape[1]
    shapes = [
        ((width_own, rows // 2), bf16),
        ((rows // 2, width_own), bf16),
        ((rows, width_own), bf16),
        ((rows, width_own), bf16),
        ((own_heads, 1, rows // 2), f32),
        ((own_heads, 5, half_block, 128), f32),
        ((3, width, width_own), bf16),
        ((width_own, width), bf16),
    ]
    return pl.pallas_call(
        attend_kernel,
        out_shape=[jax.ShapeDtypeStruct(shape, kind) for shape, kind in shapes],
        in_specs=[in_smem()] * 3 + [in_vmem()] * 9,
        out_specs=[in_vmem()] * len(shapes),
        scratch_shapes=[pltpu.VMEM((rows, lanes_step), f32)],
        compiler_params=pltpu.CompilerParams(vmem_limit_bytes=vmem_bytes),
        name="attend",
    )(me, order, table, shards, *pieces)


def attend_back(me, order, q, k, v, logs, tiles, project, grads):
    rows = k.shape[0]
    half = rows // 2
    shapes = [
        ((width_own, half), bf16),
        ((rows, width_own), bf16),
        ((rows, width_own), bf16),
        ((half, width_own), bf16),
        ((half, 2 * width_own), bf16),
        ((half, 2 * width_own), bf16),
        ((own_heads, 32, 128), f32),
    ]
    return pl.pallas_call(
        attend_back_kernel,
        out_shape=[jax.ShapeDtypeStruct(shape, kind) for shape, kind in shapes],
        in_specs=[in_smem()] * 2 + [in_vmem()] * 10,
        out_specs=[in_vmem()] * len(shapes),
        scratch_shapes=[
            pltpu.VMEM((rows, lanes_step), f32),
            pltpu.VMEM((5, half_block, 128), f32),
            pltpu.VMEM((half, width_own), bf16),
        ],
        compiler_params=pltpu.CompilerParams(vmem_limit_bytes=vmem_bytes),
        name="attend_back",
    )(me, order, q, k, v, logs, tiles, project, *grads)


def weight_pieces(me, dq, dk, dv, table, weights, attended, pieces, grads):
    rows, width = dk.shape[0], weights.shape[1]
    return pl.pallas_call(
        pieces_kernel,
        out_shape=jax.ShapeDtypeStruct((16, 136, 2 * width_own), bf16),
        in_specs=[in_smem()] + [in_vmem()] * 18,
        out_specs=in_vmem(),
        scratch_shapes=[pltpu.VMEM((rows, width), bf16)],
        compiler_params=pltpu.CompilerParams(vmem_limit_bytes=vmem_bytes),
        name="weight_pieces",
    )(me, dq, dk, dv, table, weights, attended, *pieces, *grads)


def regroup_kernel(me_ref, chunk_ref, payload_ref):
    shard_rows, wide = 24, 2 * width_own
    total = chunk_ref[0].astype(f32)
    for source in range(1, chunk_ref.shape[0]):
        total = total + chunk_ref[source].astype(f32)
    small = total[5 * shard_rows :]
    for target in range(8):
        if target < 6:
            start = (target // 2) * shard_rows
            left = (target % 2) * width_own
            part = total[start : start + shard_rows, left : left + width_own]
            part = jnp.concatenate([part, jnp.zeros((shard_rows, width_own), f32)], axis=1)
            parts = [part, jnp.zeros((shard_rows, wide), f32), small]
        else:
            mine = ((me_ref[0] % 4) // 2 == target - 6).astype(f32)
            parts = [total[3 * shard_rows : 5 * shard_rows] * mine, small]
        payload_ref[target] = jnp.concatenate(parts, axis=0).astype(bf16)


def regroup(me, chunks):
    return pl.pallas_call(
        regroup_kernel,
        out_shape=jax.ShapeDtypeStruct((8, 64, 2 * width_own), bf16),
        in_specs=[in_smem(), in_vmem()],
        out_specs=in_vmem(),
        compiler_params=pltpu.CompilerParams(vmem_limit_bytes=vmem_bytes),
        name="regroup",
    )(me, chunks)


def finish_kernel(me_ref, last_ref, gain_ref, weight_ref, table_ref, norm_ref, moe_ref, router_ref):
    shard_rows, wide = 24, 2 * width_own
    parts = [last_ref[source].astype(f32) for source in range(8)]
    as_qkv = jnp.concatenate(
        [
            parts[block][:shard_rows, :width_own] + parts[4 + block][:shard_rows, :width_own]
            for block in range(4)
        ],
        axis=1,
    )
    total = sum(parts[1:], parts[0])
    as_out = jnp.concatenate([total[:shard_rows], total[shard_rows : 2 * shard_rows]], axis=1)
    weight_ref[...] = jnp.where(me_ref[0] < 6, as_qkv, as_out)
    small = total[2 * shard_rows :]
    for head in range(table_ref.shape[0]):
        table_ref[head : head + 1] = small[0:1, head * 32 : (head + 1) * 32]
    for block in range(6):
        line, left = block // 3, (block % 3) * 128
        norm_ref[block : block + 1] = small[1 + line : 2 + line, left : left + 128]
        moe_ref[block : block + 1] = small[11 + line : 12 + line, left : left + 128]
    norm_ref[...] = norm_ref[...] / gain_ref[...]
    for block in range(4):
        early = (parts[block] + parts[4 + block])[2 * shard_rows :]
        for index in range(4):
            line = 3 + 2 * index
            router_ref[4 * block + index : 4 * block + index + 1, :wide] = early[line : line + 1]
            router_ref[4 * block + index : 4 * block + index + 1, wide:] = early[line + 1 : line + 2]


def finish(me, last, gain):
    width = gain.size
    shapes = [(24, width), (12, 32), gain.shape, gain.shape, (16, width)]
    return pl.pallas_call(
        finish_kernel,
        out_shape=[jax.ShapeDtypeStruct(shape, f32) for shape in shapes],
        in_specs=[in_smem(), in_vmem(), in_vmem()],
        out_specs=[in_vmem()] * len(shapes),
        compiler_params=pltpu.CompilerParams(vmem_limit_bytes=vmem_bytes),
        name="finish",
    )(me, last, gain)


def swap(chunks, axis):
    return lax.all_to_all(chunks, axis, split_axis=0, concat_axis=0, tiled=True)


def spread(part, axis, count):
    return swap(jnp.broadcast_to(part[None], (count,) + part.shape), axis)


def gelu(u):
    return jax.nn.gelu(u, approximate=True)


def body(
    hidden_in,
    out_grad,
    attn_norm,
    attn_weight,
    bias_table,
    moe_norm,
    router,
    expert_in,
    expert_out,
    expert_ids,
    block_order,
):
    width = attn_norm.shape[0]
    ctx_count, exp_count = 8, 16
    me = lax.axis_index("ctx")
    x_index = me % 4
    z_index = me // 4
    tokens = hidden_in.shape[1]
    expert_count = router.shape[1]
    capacity = 2 * tokens // expert_count
    me_array = me.astype(jnp.int32).reshape(1)
    order = block_order[0]

    inputs = hidden_in[0].astype(f32)
    scale_one = lax.rsqrt(jnp.mean(inputs * inputs, axis=-1, keepdims=True) + eps_norm)
    scaled_one = inputs * scale_one
    normed_low = (scaled_one * attn_norm).astype(bf16)
    pieces = [normed_low] + [
        lax.ppermute(normed_low, "ctx", gather_perm(dz, dx)) for dz, dx in offsets[1:]
    ]
    shard_rows = attn_weight.shape[0]
    by_ctx = spread(attn_weight, "ctx", ctx_count)
    qkv_own = lax.dynamic_slice_in_dim(by_ctx[:6], x_index * width_own, width_own, 2)
    out_own = lax.dynamic_index_in_dim(by_ctx, 6 + x_index // 2, 0, False)
    wide = 2 * width_own
    part_own = jnp.stack(
        [jnp.concatenate([qkv_own[2 * which], qkv_own[2 * which + 1]], axis=1) for which in range(3)]
        + [out_own[:, :wide], out_own[:, wide:]]
    )
    part_own, *pieces[1:5] = lax.optimization_barrier((part_own, *pieces[1:5]))
    by_exp = spread(part_own, "exp", exp_count)
    attended, q, k, v, logs, tiles, qkv_weights, out_weight = attend(
        me_array, order, bias_table, by_exp, pieces
    )
    out_partial = dot_tn(attended, out_weight)
    out_blocks = out_partial.reshape(4, tokens, width)
    mid = inputs + out_blocks[0]
    out_low = out_blocks.astype(bf16)
    for dx in range(1, 4):
        mid = mid + lax.ppermute(out_low[dx], "ctx", scatter_perm(0, dx)).astype(f32)

    scale_two = lax.rsqrt(jnp.mean(mid * mid, axis=-1, keepdims=True) + eps_norm)
    scaled_two = mid * scale_two
    normed_two = scaled_two * moe_norm
    logits = jnp.dot(normed_two, router, precision=highest)
    router_prob = jax.nn.softmax(logits, axis=-1)
    chosen = expert_ids[0, :, 0]
    picked = chosen[:, None] == jnp.arange(expert_count, dtype=jnp.int32)[None, :]
    gate = jnp.sum(jnp.where(picked, router_prob, 0.0), axis=-1, keepdims=True)
    earlier = (
        jnp.arange(tokens, dtype=jnp.int32)[:, None] > jnp.arange(tokens, dtype=jnp.int32)[None, :]
    )
    same = chosen[:, None] == chosen[None, :]
    slot = jnp.sum((earlier & same).astype(jnp.int32), axis=1)
    targets = chosen * capacity + slot
    placing = (
        targets[:, None] == jnp.arange(expert_count * capacity, dtype=jnp.int32)[None, :]
    ).astype(bf16)
    cotangent = out_grad[0].astype(f32)
    sent = (gate * cotangent).astype(bf16)
    both = jnp.concatenate([normed_two.astype(bf16), sent], axis=1)
    outgoing = dot_tn(placing, both).astype(bf16).reshape(exp_count, capacity, 2 * width)
    arrived = swap(outgoing, "exp").reshape(exp_count * capacity, 2 * width)

    gathered = [arrived] + [
        lax.ppermute(arrived, "ctx", gather_perm(0, dx)) for dx in range(1, 4)
    ]

    w_in, w_out = expert_in[0], expert_out[0]
    returned = swap(expert(arrived, w_in, w_out).reshape(exp_count, capacity, 2 * width), "exp")
    returned, gathered[1], gathered[3] = lax.optimization_barrier(
        (returned, gathered[1], gathered[3])
    )
    home = dot_nn(placing, returned.reshape(exp_count * capacity, 2 * width))
    expert_result, rows_back = home[:, :width], home[:, width:]

    block_out = (mid + gate * expert_result).astype(bf16)[None]
    gate_grad = jnp.sum(cotangent * expert_result, axis=-1, keepdims=True)
    prob_grad = jnp.where(picked, gate_grad, 0.0)
    logit_grad = router_prob * (
        prob_grad - jnp.sum(router_prob * prob_grad, axis=-1, keepdims=True)
    )
    router_local = lax.dot_general(
        logit_grad, normed_two, (((0,), (0,)), ((), ())), precision=highest
    )
    normed_two_grad = rows_back + lax.dot_general(
        logit_grad, router, (((1,), (1,)), ((), ())), precision=highest
    )
    moe_norm_local = jnp.sum(normed_two_grad * scaled_two, axis=0)
    gained = normed_two_grad * moe_norm
    mid_grad = cotangent + scale_two * (
        gained - scaled_two * jnp.mean(gained * scaled_two, axis=-1, keepdims=True)
    )
    attn_grad = mid_grad.astype(bf16)
    quarter = jnp.arange(width, dtype=jnp.int32)[None] // width_own
    attn_grads = []
    for dx in range(4):
        target = (x_index + dx) % 4
        small = jnp.concatenate(
            [
                lax.dynamic_slice_in_dim(router_local, target * 4, 4, 0),
                jnp.where(quarter == target, moe_norm_local[None], 0.0),
                jnp.zeros((11, width), f32),
            ],
            axis=0,
        )
        part = jnp.concatenate([attn_grad, small.astype(bf16)], axis=0)
        attn_grads.append(lax.ppermute(part, "ctx", gather_perm(0, dx)) if dx else part)

    in_columns, out_own_grad, out_other_grad = expert_grads(
        me_array, gathered, w_in, w_out
    )
    in_columns, *attn_grads = lax.optimization_barrier((in_columns, *attn_grads))
    columns_last = swap(in_columns, "ctx")
    dq, dk, dv, query_grad, kept, given, table_local = attend_back(
        me_array, order, q, k, v, logs, tiles, out_weight, attn_grads
    )
    taken = lax.ppermute(given, "ctx", gather_perm(1, 0))
    chunks = weight_pieces(
        me_array, dq, dk, dv, table_local, qkv_weights, attended, pieces, attn_grads
    )
    chunks, taken, columns_last = lax.optimization_barrier((chunks, taken, columns_last))
    payload = regroup(me_array, swap(chunks, "exp"))

    normed_grad, *row_low = rows_grad(query_grad, kept, taken, qkv_weights)
    row_parts = [
        lax.ppermute(low_part, "ctx", scatter_perm(0, index + 1))
        for index, low_part in enumerate(row_low)
    ]
    *row_parts, _ = lax.optimization_barrier((*row_parts, payload[0, :1, :1]))
    for part in row_parts:
        normed_grad = normed_grad + part.astype(f32)
    out_other_grad, _ = lax.optimization_barrier((out_other_grad, payload[0, :1, :1]))
    out_taken = lax.ppermute(out_other_grad, "ctx", gather_perm(1, 0))
    expert_in_grad = place(columns_last)
    expert_out_grad = (out_own_grad + out_taken.astype(f32))[None]
    gained_one = normed_grad * attn_norm
    input_grad = (
        mid_grad
        + scale_one
        * (gained_one - scaled_one * jnp.mean(gained_one * scaled_one, axis=-1, keepdims=True))
    )[None]

    attn_weight_grad, table_row, norm_row, moe_row, router_rows = finish(
        me_array, swap(payload, "ctx"), attn_norm.reshape(-1, 128)
    )
    bias_table_grad = table_row.T
    attn_norm_grad = norm_row.reshape(-1)
    moe_norm_grad = moe_row.reshape(-1)
    router_grad = router_rows.T
    return (
        block_out,
        input_grad,
        attn_norm_grad,
        attn_weight_grad,
        bias_table_grad,
        moe_norm_grad,
        router_grad,
        expert_in_grad[None],
        expert_out_grad,
    )


def solution(mesh):
    placed = (
        P("exp", "ctx", None),
        P("exp", "ctx", None),
        P(),
        P(("ctx", "exp"), None),
        P(),
        P(),
        P(),
        P("exp", None, None),
        P("exp", None, None),
        P("exp", "ctx", None),
        P("exp", None),
    )
    return jax.shard_map(
        body,
        mesh=mesh,
        in_specs=placed,
        out_specs=(
            P("exp", "ctx", None),
            P("exp", "ctx", None),
            P(),
            P(("ctx", "exp"), None),
            P(),
            P(),
            P(),
            P("exp", "ctx", None),
            P("exp", "ctx", None),
        ),
        check_vma=False,
    )
```

```python
from functools import partial
import math

import jax
import jax.numpy as jnp
from jax import lax
from jax.experimental import pallas as pl
from jax.experimental.pallas import tpu as pltpu
from jax.sharding import PartitionSpec as P

f32 = jnp.float32
bf16 = jnp.bfloat16
eps_norm = 1e-06
highest = lax.Precision.HIGHEST
bucket_edges = [
    edge if edge <= 16 else int(math.ceil(16.0 * 8.0 ** ((edge - 16) / 16.0)))
    for edge in range(1, 32)
]
masked = -1e30
head_size = 64
own_heads = 3
width_own = own_heads * head_size
half_block = 64
block_count = 16
query_blocks = 8
lanes_step = 256
vmem_bytes = 56 * 1024 * 1024

offsets = [(dz, dx) for dz in range(2) for dx in range(4)]


def gather_perm(dz, dx):
    return [(4 * z + x, 4 * (z ^ dz) + (x + dx) % 4) for z in range(2) for x in range(4)]


def scatter_perm(dz, dx):
    return [(4 * z + x, 4 * (z ^ dz) + (x - dx) % 4) for z in range(2) for x in range(4)]


def dot_nt(left, right):
    return lax.dot_general(left, right, (((1,), (1,)), ((), ())), preferred_element_type=f32)


def dot_tn(left, right):
    return lax.dot_general(left, right, (((0,), (0,)), ((), ())), preferred_element_type=f32)


def dot_nn(left, right):
    return jnp.dot(left, right, preferred_element_type=f32)


def block_places(me_ref, order_ref):
    me = me_ref[0]
    z, x = me // 4, me % 4
    places = []
    for dz, dx in offsets:
        source = 4 * ((z + dz) % 2) + (x - dx + 4) % 4
        places += [order_ref[2 * source], order_ref[2 * source + 1]]
    return places


def tile_class(places, query_block, key_block):
    return jnp.clip(places[query_block] - places[key_block], -1, 3) + 1


def tile_distance(step):
    key_row = lax.broadcasted_iota(jnp.int32, (half_block, 128), 0)
    query_row = lax.broadcasted_iota(jnp.int32, (half_block, 128), 1) & (half_block - 1)
    return step * half_block + query_row - key_row


def attend_kernel(me_ref, order_ref, table_ref, shards_ref, *refs):
    pieces, refs = refs[:8], refs[8:]
    out_ref, q_ref, k_ref, v_ref, log_ref, tiles_ref, weight_ref, project_ref, scores_ref = refs
    exp_count = shards_ref.shape[0]
    for which in range(3):
        weight_ref[which] = jnp.concatenate(
            [
                shards_ref[piece, which].astype(f32)[:, part * width_own : (part + 1) * width_own]
                for part in range(2)
                for piece in range(exp_count)
            ],
            axis=0,
        ).astype(bf16)
    first_piece = (me_ref[0] % 2) * (exp_count // 2)
    for part in range(2):
        project_ref[:, part * 2 * width_own : (part + 1) * 2 * width_own] = jnp.concatenate(
            [
                shards_ref[first_piece + piece, 3 + part].astype(f32)
                for piece in range(exp_count // 2)
            ],
            axis=0,
        ).astype(bf16)
    places = block_places(me_ref, order_ref)
    first_head = (me_ref[0] % 4) * own_heads
    for head in range(own_heads):
        tiles_ref[head, 0] = jnp.full((half_block, 128), masked, f32)
        tiles_ref[head, 4] = jnp.full((half_block, 128), table_ref[31, first_head + head], f32)
    for step in range(3):
        distance = tile_distance(step)
        terms = [
            jnp.full((half_block, 128), table_ref[0, first_head + head], f32)
            for head in range(own_heads)
        ]
        for bucket, edge in enumerate(bucket_edges, 1):
            beyond = distance >= edge
            for head in range(own_heads):
                terms[head] = jnp.where(beyond, table_ref[bucket, first_head + head], terms[head])
        for head in range(own_heads):
            tiles_ref[head, step + 1] = (
                jnp.where(distance >= 0, terms[head], masked) if step == 0 else terms[head]
            )
    for index, piece in enumerate(pieces):
        rows = slice(index * piece.shape[0], (index + 1) * piece.shape[0])
        normed = piece[...]
        k_ref[rows] = dot_nn(normed, weight_ref[1]).astype(bf16)
        v_ref[rows] = dot_nn(normed, weight_ref[2]).astype(bf16)
        if index < 4:
            q_ref[rows] = dot_nn(normed, weight_ref[0]).astype(bf16) * bf16(0.125)
    first_half = lax.broadcasted_iota(jnp.int32, (half_block, 128), 1) < half_block
    for head in range(own_heads):
        columns = slice(head * head_size, (head + 1) * head_size)
        keys, values = k_ref[:, columns], v_ref[:, columns]
        for part in range(query_blocks * half_block // lanes_step):
            lanes = slice(part * lanes_step, (part + 1) * lanes_step)
            add_bias(places, tiles_ref, scores_ref, first_half, head, part,
                     dot_nt(keys, q_ref[lanes, columns]))
            scores = scores_ref[...]
            peak = jnp.max(scores, axis=0, keepdims=True)
            raised = jnp.exp(scores - peak)
            total = jnp.sum(raised, axis=0, keepdims=True)
            probs = (raised * (1.0 / total)).astype(bf16)
            out_ref[columns, lanes] = dot_tn(values, probs).astype(bf16)
            log_ref[head, :, lanes] = peak + jnp.log(total)


def add_bias(places, tiles_ref, scores_ref, first_half, head, part, raw):
    for key_block in range(block_count):
        rows = slice(key_block * half_block, (key_block + 1) * half_block)
        for group in range(lanes_step // 128):
            lanes = slice(group * 128, (group + 1) * 128)
            query_block = part * (lanes_step // half_block) + 2 * group
            left = tile_class(places, query_block, key_block)
            right = tile_class(places, query_block + 1, key_block)
            scores_ref[rows, lanes] = raw[rows, lanes] + jnp.where(
                first_half, tiles_ref[head, left], tiles_ref[head, right]
            )


def attend_back_kernel(
    me_ref, order_ref, q_ref, k_ref, v_ref, log_ref, tiles_ref, project_ref, *refs,
):
    grad_pieces, refs = refs[:4], refs[4:]
    dq_ref, dk_ref, dv_ref, query_ref, keep_ref, give_ref, table_ref = refs[:7]
    scores_ref, sums_ref, grad_ref = refs[7:]
    places = block_places(me_ref, order_ref)
    size = query_blocks * half_block // 4
    for index, piece in enumerate(grad_pieces):
        rows = slice(index * size, (index + 1) * size)
        grad_ref[rows] = dot_nt(piece[:size], project_ref[...]).astype(bf16)
    first_half = lax.broadcasted_iota(jnp.int32, (half_block, 128), 1) < half_block
    buckets = []
    for step in range(3):
        distance = tile_distance(step)
        counted = jnp.zeros((half_block, 128), jnp.int32)
        for edge in bucket_edges:
            counted = counted + (distance >= edge).astype(jnp.int32)
        buckets.append(counted)
    for head in range(own_heads):
        columns = slice(head * head_size, (head + 1) * head_size)
        keys, values = k_ref[:, columns], v_ref[:, columns]
        sums_ref[...] = jnp.zeros_like(sums_ref)
        key_sum = value_sum = None
        for part in range(query_blocks * half_block // lanes_step):
            lanes = slice(part * lanes_step, (part + 1) * lanes_step)
            queries, grads = q_ref[lanes, columns], grad_ref[lanes, columns]
            add_bias(places, tiles_ref, scores_ref, first_half, head, part, dot_nt(keys, queries))
            probs = jnp.exp(scores_ref[...] - log_ref[head, :, lanes])
            probs_grad = dot_nt(values, grads)
            row_dot = jnp.sum(probs * probs_grad, axis=0, keepdims=True)
            score_grad = probs * (probs_grad - row_dot)
            scores_ref[...] = score_grad
            low = score_grad.astype(bf16)
            value_part = dot_nn(probs.astype(bf16), grads)
            key_part = dot_nn(low, queries)
            value_sum = value_part if value_sum is None else value_sum + value_part
            key_sum = key_part if key_sum is None else key_sum + key_part
            dq_ref[columns, lanes] = (dot_tn(keys, low) * 0.125).astype(bf16)
            for key_block in range(block_count):
                rows = slice(key_block * half_block, (key_block + 1) * half_block)
                for group in range(lanes_step // 128):
                    query_block = part * (lanes_step // half_block) + 2 * group
                    left = tile_class(places, query_block, key_block)
                    right = tile_class(places, query_block + 1, key_block)
                    tile = scores_ref[rows, group * 128 : (group + 1) * 128]
                    sums_ref[left] += jnp.where(first_half, tile, 0.0)
                    sums_ref[right] += jnp.where(first_half, 0.0, tile)
        dk_ref[:, columns] = key_sum.astype(bf16)
        dv_ref[:, columns] = value_sum.astype(bf16)
        for bucket in range(32):
            found = [jnp.where(buckets[step] == bucket, sums_ref[step + 1], 0.0) for step in range(3)]
            if bucket == 31:
                found.append(sums_ref[4])
            table_ref[head, bucket : bucket + 1, :] = jnp.sum(sum(found), axis=0, keepdims=True)

    dq, dk, dv = dq_ref[...], dk_ref[...], dv_ref[...]
    half = query_blocks * half_block
    query_ref[...] = dq.T
    keys_values = jnp.concatenate([dk.astype(f32), dv.astype(f32)], axis=1).astype(bf16)
    keep_ref[...] = keys_values[:half]
    give_ref[...] = keys_values[half:]


def pieces_kernel(
    me_ref, dq_ref, dk_ref, dv_ref, table_ref, weight_ref, attended_ref, *refs,
):
    pieces, grad_pieces, chunk_ref, normed_ref = refs[:8], refs[8:12], refs[12], refs[13]
    size = pieces[0].shape[0]
    for index, piece in enumerate(pieces):
        normed_ref[index * size : (index + 1) * size] = piece[...]
    project_grad = jnp.zeros((width_own, normed_ref.shape[1]), f32)
    for index, piece in enumerate(grad_pieces):
        rows = slice(index * size, (index + 1) * size)
        project_grad = project_grad + dot_nn(attended_ref[:, rows], piece[:size])
    normed = normed_ref[...]
    half = normed.shape[0] // 2
    exp_count = chunk_ref.shape[0]
    shard_rows = 24
    flipped = [
        dot_nn(dq_ref[...], normed[:half]),
        dot_tn(dk_ref[...], normed),
        dot_tn(dv_ref[...], normed),
    ]
    norm_sum = jnp.zeros((1, normed.shape[1]), f32)
    straight = []
    for which in range(3):
        weight_t = weight_ref[which].astype(f32).T
        norm_sum = norm_sum + jnp.sum(flipped[which] * weight_t, axis=0, keepdims=True)
        straight.append(flipped[which].T)
    wide = 2 * width_own
    row = lax.broadcasted_iota(jnp.int32, (16, wide), 0)
    heads = [jnp.sum(table_ref[head].T, axis=0, keepdims=True) for head in range(own_heads)]
    table_row = jnp.concatenate(
        [
            heads[head] * (me_ref[0] % 4 == group).astype(f32)
            for group in range(4)
            for head in range(own_heads)
        ],
        axis=1,
    )
    small_rows = [table_row, norm_sum[:, :wide], norm_sum[:, wide:]]
    early = sum(piece[size:].astype(f32) for piece in grad_pieces)
    for index in range(5):
        for block in range(2):
            small_rows.append(early[index : index + 1, block * wide : (block + 1) * wide])
    small_slab = jnp.zeros((16, wide), f32)
    for index, small_row in enumerate(small_rows):
        small_slab = jnp.where(row == index, small_row, small_slab)
    odd = me_ref[0] % 2
    for piece in range(exp_count):
        slabs = []
        for which in range(3):
            starts = [(part * exp_count + piece) * shard_rows for part in range(2)]
            slabs.append(
                jnp.concatenate(
                    [straight[which][start : start + shard_rows] for start in starts], axis=1
                )
            )
        start = (piece % 8) * shard_rows
        mine = (odd == piece // 8).astype(f32)
        for block in range(2):
            slabs.append(
                project_grad[start : start + shard_rows, block * wide : (block + 1) * wide] * mine
            )
        chunk_ref[piece] = jnp.concatenate(slabs + [small_slab], axis=0).astype(bf16)


def rows_kernel(query_ref, keep_ref, taken_ref, weight_ref, own_ref, *low_refs):
    size = own_ref.shape[0]
    for index in range(4):
        rows = slice(index * size, (index + 1) * size)
        both = keep_ref[rows].astype(f32) + taken_ref[rows].astype(f32)
        part = dot_nt(query_ref[rows], weight_ref[0])
        part = part + dot_nt(both[:, :width_own].astype(bf16), weight_ref[1])
        part = part + dot_nt(both[:, width_own:].astype(bf16), weight_ref[2])
        if index:
            low_refs[index - 1][...] = part.astype(bf16)
        else:
            own_ref[...] = part


def rows_grad(query, keep, taken, weights):
    size, width = query.shape[0] // 4, weights.shape[1]
    return pl.pallas_call(
        rows_kernel,
        out_shape=[jax.ShapeDtypeStruct((size, width), kind) for kind in (f32, bf16, bf16, bf16)],
        in_specs=[in_vmem()] * 4,
        out_specs=[in_vmem()] * 4,
        compiler_params=pltpu.CompilerParams(vmem_limit_bytes=vmem_bytes),
        name="rows_grad",
    )(query, keep, taken, weights)


def place_kernel(columns_ref, placed_ref):
    tile = columns_ref.shape[2] // 2
    for source in range(4):
        both = columns_ref[source].astype(f32) + columns_ref[4 + source].astype(f32)
        for part in range(2):
            start = (4 * part + source) * tile
            placed_ref[:, start : start + tile] = both[:, part * tile : (part + 1) * tile]


def place(columns):
    count, rows, double = columns.shape
    return pl.pallas_call(
        place_kernel,
        out_shape=jax.ShapeDtypeStruct((rows, count * double // 2), f32),
        in_specs=[in_vmem()],
        out_specs=in_vmem(),
        compiler_params=pltpu.CompilerParams(vmem_limit_bytes=vmem_bytes),
        name="place",
    )(columns)


def gelu_both(u):
    slope = math.sqrt(2.0 / math.pi)
    square = u * u
    bent = jnp.tanh(slope * u * (1.0 + 0.044715 * square))
    halved = 0.5 * (1.0 + bent)
    derivative = halved + 0.5 * u * (1.0 - bent * bent) * (slope * (1.0 + 0.134145 * square))
    return u * halved, derivative


def expert_kernel(rows_ref, in_ref, out_ref, result_ref, sum_ref):
    step = pl.program_id(0)
    width = in_ref.shape[0]
    rows_in, rows_grad = rows_ref[:, :width], rows_ref[:, width:]
    hidden, derivative = gelu_both(dot_nn(rows_in, in_ref[...]))
    produced = dot_nn(hidden.astype(bf16), out_ref[...])
    pre_grad = (dot_nt(rows_grad, out_ref[...]) * derivative).astype(bf16)
    row_grad = dot_nt(pre_grad, in_ref[...])

    @pl.when(step == 0)
    def _():
        sum_ref[:, :width] = produced
        sum_ref[:, width:] = row_grad

    @pl.when(step > 0)
    def _():
        sum_ref[:, :width] += produced
        sum_ref[:, width:] += row_grad

    @pl.when(step == pl.num_programs(0) - 1)
    def _():
        result_ref[...] = sum_ref[...].astype(bf16)


def expert(rows, w_in, w_out):
    count, double = rows.shape
    width, hidden = w_in.shape
    tile = hidden // 3
    return pl.pallas_call(
        expert_kernel,
        grid=(3,),
        out_shape=jax.ShapeDtypeStruct((count, double), bf16),
        in_specs=[
            pl.BlockSpec((count, double), lambda i: (0, 0)),
            pl.BlockSpec((width, tile), lambda i: (0, i)),
            pl.BlockSpec((tile, width), lambda i: (i, 0)),
        ],
        out_specs=pl.BlockSpec((count, double), lambda i: (0, 0)),
        scratch_shapes=[pltpu.VMEM((count, double), f32)],
        compiler_params=pltpu.CompilerParams(vmem_limit_bytes=vmem_bytes),
        name="expert",
    )(rows, w_in, w_out)


def expert_grads_kernel(
    me_ref, rows_a, rows_b, rows_c, rows_d, in_ref, out_ref,
    columns_ref, own_ref, other_ref,
):
    step = pl.program_id(0)
    width = in_ref.shape[0]
    in_sum = out_sum = None
    for piece in (rows_a, rows_b, rows_c, rows_d):
        rows_in, rows_grad = piece[:, :width], piece[:, width:]
        hidden, derivative = gelu_both(dot_nn(rows_in, in_ref[...]))
        pre_grad = (dot_nt(rows_grad, out_ref[...]) * derivative).astype(bf16)
        out_part = dot_tn(hidden.astype(bf16), rows_grad)
        in_part = dot_tn(rows_in, pre_grad)
        out_sum = out_part if out_sum is None else out_sum + out_part
        in_sum = in_part if in_sum is None else in_sum + in_part
    count = columns_ref.shape[0]
    in_rows = width // count
    columns_ref[...] = in_sum.astype(bf16).reshape(count, in_rows, in_sum.shape[1])

    @pl.when(step == me_ref[0] // 4)
    def _():
        own_ref[...] = out_sum

    @pl.when(step != me_ref[0] // 4)
    def _():
        other_ref[...] = out_sum.astype(bf16)


def expert_grads(me, pieces, w_in, w_out):
    count, double = pieces[0].shape
    width, hidden = w_in.shape
    tile = hidden // 8
    in_rows = width // 8
    return pl.pallas_call(
        expert_grads_kernel,
        grid_spec=pltpu.PrefetchScalarGridSpec(
            num_scalar_prefetch=1,
            grid=(2,),
            in_specs=[pl.BlockSpec((count, double), lambda i, me: (0, 0))] * 4
            + [
                pl.BlockSpec((width, tile), lambda i, me: (0, 4 * i + me[0] % 4)),
                pl.BlockSpec((tile, width), lambda i, me: (4 * i + me[0] % 4, 0)),
            ],
            out_specs=[
                pl.BlockSpec((8, in_rows, tile), lambda i, me: (0, 0, i)),
                pl.BlockSpec((tile, width), lambda i, me: (0, 0)),
                pl.BlockSpec((tile, width), lambda i, me: (0, 0)),
            ],
        ),
        out_shape=[
            jax.ShapeDtypeStruct((8, in_rows, 2 * tile), bf16),
            jax.ShapeDtypeStruct((tile, width), f32),
            jax.ShapeDtypeStruct((tile, width), bf16),
        ],
        compiler_params=pltpu.CompilerParams(vmem_limit_bytes=vmem_bytes),
        name="expert_grads",
    )(me, *pieces, w_in, w_out)


def in_smem():
    return pl.BlockSpec(memory_space=pltpu.SMEM)


def in_vmem():
    return pl.BlockSpec(memory_space=pltpu.VMEM)


def attend(me, order, table, shards, pieces):
    rows = 8 * pieces[0].shape[0]
    width = pieces[0].shape[1]
    shapes = [
        ((width_own, rows // 2), bf16),
        ((rows // 2, width_own), bf16),
        ((rows, width_own), bf16),
        ((rows, width_own), bf16),
        ((own_heads, 1, rows // 2), f32),
        ((own_heads, 5, half_block, 128), f32),
        ((3, width, width_own), bf16),
        ((width_own, width), bf16),
    ]
    return pl.pallas_call(
        attend_kernel,
        out_shape=[jax.ShapeDtypeStruct(shape, kind) for shape, kind in shapes],
        in_specs=[in_smem()] * 3 + [in_vmem()] * 9,
        out_specs=[in_vmem()] * len(shapes),
        scratch_shapes=[pltpu.VMEM((rows, lanes_step), f32)],
        compiler_params=pltpu.CompilerParams(vmem_limit_bytes=vmem_bytes),
        name="attend",
    )(me, order, table, shards, *pieces)


def attend_back(me, order, q, k, v, logs, tiles, project, grads):
    rows = k.shape[0]
    half = rows // 2
    shapes = [
        ((width_own, half), bf16),
        ((rows, width_own), bf16),
        ((rows, width_own), bf16),
        ((half, width_own), bf16),
        ((half, 2 * width_own), bf16),
        ((half, 2 * width_own), bf16),
        ((own_heads, 32, 128), f32),
    ]
    return pl.pallas_call(
        attend_back_kernel,
        out_shape=[jax.ShapeDtypeStruct(shape, kind) for shape, kind in shapes],
        in_specs=[in_smem()] * 2 + [in_vmem()] * 10,
        out_specs=[in_vmem()] * len(shapes),
        scratch_shapes=[
            pltpu.VMEM((rows, lanes_step), f32),
            pltpu.VMEM((5, half_block, 128), f32),
            pltpu.VMEM((half, width_own), bf16),
        ],
        compiler_params=pltpu.CompilerParams(vmem_limit_bytes=vmem_bytes),
        name="attend_back",
    )(me, order, q, k, v, logs, tiles, project, *grads)


def weight_pieces(me, dq, dk, dv, table, weights, attended, pieces, grads):
    rows, width = dk.shape[0], weights.shape[1]
    return pl.pallas_call(
        pieces_kernel,
        out_shape=jax.ShapeDtypeStruct((16, 136, 2 * width_own), bf16),
        in_specs=[in_smem()] + [in_vmem()] * 18,
        out_specs=in_vmem(),
        scratch_shapes=[pltpu.VMEM((rows, width), bf16)],
        compiler_params=pltpu.CompilerParams(vmem_limit_bytes=vmem_bytes),
        name="weight_pieces",
    )(me, dq, dk, dv, table, weights, attended, *pieces, *grads)


def regroup_kernel(me_ref, chunk_ref, payload_ref):
    shard_rows, wide = 24, 2 * width_own
    total = chunk_ref[0].astype(f32)
    for source in range(1, chunk_ref.shape[0]):
        total = total + chunk_ref[source].astype(f32)
    small = total[5 * shard_rows :]
    for target in range(8):
        if target < 6:
            start = (target // 2) * shard_rows
            left = (target % 2) * width_own
            part = total[start : start + shard_rows, left : left + width_own]
            part = jnp.concatenate([part, jnp.zeros((shard_rows, width_own), f32)], axis=1)
            parts = [part, jnp.zeros((shard_rows, wide), f32), small]
        else:
            mine = ((me_ref[0] % 4) // 2 == target - 6).astype(f32)
            parts = [total[3 * shard_rows : 5 * shard_rows] * mine, small]
        payload_ref[target] = jnp.concatenate(parts, axis=0).astype(bf16)


def regroup(me, chunks):
    return pl.pallas_call(
        regroup_kernel,
        out_shape=jax.ShapeDtypeStruct((8, 64, 2 * width_own), bf16),
        in_specs=[in_smem(), in_vmem()],
        out_specs=in_vmem(),
        compiler_params=pltpu.CompilerParams(vmem_limit_bytes=vmem_bytes),
        name="regroup",
    )(me, chunks)


def finish_kernel(me_ref, last_ref, gain_ref, weight_ref, table_ref, norm_ref, moe_ref, router_ref):
    shard_rows, wide = 24, 2 * width_own
    parts = [last_ref[source].astype(f32) for source in range(8)]
    as_qkv = jnp.concatenate(
        [
            parts[block][:shard_rows, :width_own] + parts[4 + block][:shard_rows, :width_own]
            for block in range(4)
        ],
        axis=1,
    )
    total = sum(parts[1:], parts[0])
    as_out = jnp.concatenate([total[:shard_rows], total[shard_rows : 2 * shard_rows]], axis=1)
    weight_ref[...] = jnp.where(me_ref[0] < 6, as_qkv, as_out)
    small = total[2 * shard_rows :]
    for head in range(table_ref.shape[0]):
        table_ref[head : head + 1] = small[0:1, head * 32 : (head + 1) * 32]
    for block in range(6):
        line, left = block // 3, (block % 3) * 128
        norm_ref[block : block + 1] = small[1 + line : 2 + line, left : left + 128]
        moe_ref[block : block + 1] = small[11 + line : 12 + line, left : left + 128]
    norm_ref[...] = norm_ref[...] / gain_ref[...]
    for block in range(4):
        early = (parts[block] + parts[4 + block])[2 * shard_rows :]
        for index in range(4):
            line = 3 + 2 * index
            router_ref[4 * block + index : 4 * block + index + 1, :wide] = early[line : line + 1]
            router_ref[4 * block + index : 4 * block + index + 1, wide:] = early[line + 1 : line + 2]


def finish(me, last, gain):
    width = gain.size
    shapes = [(24, width), (12, 32), gain.shape, gain.shape, (16, width)]
    return pl.pallas_call(
        finish_kernel,
        out_shape=[jax.ShapeDtypeStruct(shape, f32) for shape in shapes],
        in_specs=[in_smem(), in_vmem(), in_vmem()],
        out_specs=[in_vmem()] * len(shapes),
        compiler_params=pltpu.CompilerParams(vmem_limit_bytes=vmem_bytes),
        name="finish",
    )(me, last, gain)


def swap(chunks, axis):
    return lax.all_to_all(chunks, axis, split_axis=0, concat_axis=0, tiled=True)


def spread(part, axis, count):
    return swap(jnp.broadcast_to(part[None], (count,) + part.shape), axis)


def gelu(u):
    return jax.nn.gelu(u, approximate=True)


def body(
    hidden_in,
    out_grad,
    attn_norm,
    attn_weight,
    bias_table,
    moe_norm,
    router,
    expert_in,
    expert_out,
    expert_ids,
    block_order,
):
    width = attn_norm.shape[0]
    ctx_count, exp_count = 8, 16
    me = lax.axis_index("ctx")
    x_index = me % 4
    z_index = me // 4
    tokens = hidden_in.shape[1]
    expert_count = router.shape[1]
    capacity = 2 * tokens // expert_count
    me_array = me.astype(jnp.int32).reshape(1)
    order = block_order[0]

    inputs = hidden_in[0].astype(f32)
    scale_one = lax.rsqrt(jnp.mean(inputs * inputs, axis=-1, keepdims=True) + eps_norm)
    scaled_one = inputs * scale_one
    normed_low = (scaled_one * attn_norm).astype(bf16)
    pieces = [normed_low] + [
        lax.ppermute(normed_low, "ctx", gather_perm(dz, dx)) for dz, dx in offsets[1:]
    ]
    shard_rows = attn_weight.shape[0]
    by_ctx = spread(attn_weight, "ctx", ctx_count)
    qkv_own = lax.dynamic_slice_in_dim(by_ctx[:6], x_index * width_own, width_own, 2)
    out_own = lax.dynamic_index_in_dim(by_ctx, 6 + x_index // 2, 0, False)
    wide = 2 * width_own
    part_own = jnp.stack(
        [jnp.concatenate([qkv_own[2 * which], qkv_own[2 * which + 1]], axis=1) for which in range(3)]
        + [out_own[:, :wide], out_own[:, wide:]]
    )
    part_own, *pieces[1:5] = lax.optimization_barrier((part_own, *pieces[1:5]))
    by_exp = spread(part_own, "exp", exp_count)
    attended, q, k, v, logs, tiles, qkv_weights, out_weight = attend(
        me_array, order, bias_table, by_exp, pieces
    )
    out_partial = dot_tn(attended, out_weight)
    out_blocks = out_partial.reshape(4, tokens, width)
    mid = inputs + out_blocks[0]
    out_low = out_blocks.astype(bf16)
    for dx in range(1, 4):
        mid = mid + lax.ppermute(out_low[dx], "ctx", scatter_perm(0, dx)).astype(f32)

    scale_two = lax.rsqrt(jnp.mean(mid * mid, axis=-1, keepdims=True) + eps_norm)
    scaled_two = mid * scale_two
    normed_two = scaled_two * moe_norm
    logits = jnp.dot(normed_two, router, precision=highest)
    router_prob = jax.nn.softmax(logits, axis=-1)
    chosen = expert_ids[0, :, 0]
    picked = chosen[:, None] == jnp.arange(expert_count, dtype=jnp.int32)[None, :]
    gate = jnp.sum(jnp.where(picked, router_prob, 0.0), axis=-1, keepdims=True)
    earlier = (
        jnp.arange(tokens, dtype=jnp.int32)[:, None] > jnp.arange(tokens, dtype=jnp.int32)[None, :]
    )
    same = chosen[:, None] == chosen[None, :]
    slot = jnp.sum((earlier & same).astype(jnp.int32), axis=1)
    targets = chosen * capacity + slot
    placing = (
        targets[:, None] == jnp.arange(expert_count * capacity, dtype=jnp.int32)[None, :]
    ).astype(bf16)
    cotangent = out_grad[0].astype(f32)
    sent = (gate * cotangent).astype(bf16)
    both = jnp.concatenate([normed_two.astype(bf16), sent], axis=1)
    outgoing = dot_tn(placing, both).astype(bf16).reshape(exp_count, capacity, 2 * width)
    arrived = swap(outgoing, "exp").reshape(exp_count * capacity, 2 * width)

    gathered = [arrived] + [
        lax.ppermute(arrived, "ctx", gather_perm(0, dx)) for dx in range(1, 4)
    ]

    w_in, w_out = expert_in[0], expert_out[0]
    returned = swap(expert(arrived, w_in, w_out).reshape(exp_count, capacity, 2 * width), "exp")
    returned, gathered[1], gathered[3] = lax.optimization_barrier(
        (returned, gathered[1], gathered[3])
    )
    home = dot_nn(placing, returned.reshape(exp_count * capacity, 2 * width))
    expert_result, rows_back = home[:, :width], home[:, width:]

    block_out = (mid + gate * expert_result).astype(bf16)[None]
    gate_grad = jnp.sum(cotangent * expert_result, axis=-1, keepdims=True)
    prob_grad = jnp.where(picked, gate_grad, 0.0)
    logit_grad = router_prob * (
        prob_grad - jnp.sum(router_prob * prob_grad, axis=-1, keepdims=True)
    )
    router_local = lax.dot_general(
        logit_grad, normed_two, (((0,), (0,)), ((), ())), precision=highest
    )
    normed_two_grad = rows_back + lax.dot_general(
        logit_grad, router, (((1,), (1,)), ((), ())), precision=highest
    )
    moe_norm_local = jnp.sum(normed_two_grad * scaled_two, axis=0)
    gained = normed_two_grad * moe_norm
    mid_grad = cotangent + scale_two * (
        gained - scaled_two * jnp.mean(gained * scaled_two, axis=-1, keepdims=True)
    )
    attn_grad = mid_grad.astype(bf16)
    quarter = jnp.arange(width, dtype=jnp.int32)[None] // width_own
    attn_grads = []
    for dx in range(4):
        target = (x_index + dx) % 4
        small = jnp.concatenate(
            [
                lax.dynamic_slice_in_dim(router_local, target * 4, 4, 0),
                jnp.where(quarter == target, moe_norm_local[None], 0.0),
                jnp.zeros((11, width), f32),
            ],
            axis=0,
        )
        part = jnp.concatenate([attn_grad, small.astype(bf16)], axis=0)
        attn_grads.append(lax.ppermute(part, "ctx", gather_perm(0, dx)) if dx else part)

    in_columns, out_own_grad, out_other_grad = expert_grads(
        me_array, gathered, w_in, w_out
    )
    in_columns, *attn_grads = lax.optimization_barrier((in_columns, *attn_grads))
    columns_last = swap(in_columns, "ctx")
    dq, dk, dv, query_grad, kept, given, table_local = attend_back(
        me_array, order, q, k, v, logs, tiles, out_weight, attn_grads
    )
    taken = lax.ppermute(given, "ctx", gather_perm(1, 0))
    chunks = weight_pieces(
        me_array, dq, dk, dv, table_local, qkv_weights, attended, pieces, attn_grads
    )
    chunks, taken, columns_last = lax.optimization_barrier((chunks, taken, columns_last))
    collected = swap(chunks, "exp")
    out_other_grad, _ = lax.optimization_barrier((out_other_grad, collected[0, :1, :1]))
    out_taken = lax.ppermute(out_other_grad, "ctx", gather_perm(1, 0))
    payload = regroup(me_array, collected)

    normed_grad, *row_low = rows_grad(query_grad, kept, taken, qkv_weights)
    row_parts = [
        lax.ppermute(low_part, "ctx", scatter_perm(0, index + 1))
        for index, low_part in enumerate(row_low)
    ]
    *row_parts, _ = lax.optimization_barrier((*row_parts, payload[0, :1, :1]))
    for part in row_parts:
        normed_grad = normed_grad + part.astype(f32)
    expert_in_grad = place(columns_last)
    gained_one = normed_grad * attn_norm
    input_grad = (
        mid_grad
        + scale_one
        * (gained_one - scaled_one * jnp.mean(gained_one * scaled_one, axis=-1, keepdims=True))
    )[None]

    last = swap(payload, "ctx")
    last, out_taken = lax.optimization_barrier((last, out_taken))
    expert_out_grad = (out_own_grad + out_taken.astype(f32))[None]
    attn_weight_grad, table_row, norm_row, moe_row, router_rows = finish(
        me_array, last, attn_norm.reshape(-1, 128)
    )
    bias_table_grad = table_row.T
    attn_norm_grad = norm_row.reshape(-1)
    moe_norm_grad = moe_row.reshape(-1)
    router_grad = router_rows.T
    return (
        block_out,
        input_grad,
        attn_norm_grad,
        attn_weight_grad,
        bias_table_grad,
        moe_norm_grad,
        router_grad,
        expert_in_grad[None],
        expert_out_grad,
    )


def solution(mesh):
    placed = (
        P("exp", "ctx", None),
        P("exp", "ctx", None),
        P(),
        P(("ctx", "exp"), None),
        P(),
        P(),
        P(),
        P("exp", None, None),
        P("exp", None, None),
        P("exp", "ctx", None),
        P("exp", None),
    )
    return jax.shard_map(
        body,
        mesh=mesh,
        in_specs=placed,
        out_specs=(
            P("exp", "ctx", None),
            P("exp", "ctx", None),
            P(),
            P(("ctx", "exp"), None),
            P(),
            P(),
            P(),
            P("exp", "ctx", None),
            P("exp", "ctx", None),
        ),
        check_vma=False,
    )
```
